128 devices in a mesh: vert: 128 (over y, x, z, core).
Axes of the slice: x: 4, y: 4, z: 4, core: 2. Of those that a mesh axis runs over, the one named last changes fastest.
Arguments:
- features: bfloat16 [131072, 512], P('vert'), may hold values from -6 to 6
- send_rows: int32 [128, 128, 4], P('vert'), may hold values from 0 to 1023
- mirror_count: int32 [128, 128], P('vert'), may hold values from 1 to 4, as said below
- tile_coord: int32 [128, 2, 128], P('vert'), may hold values from 0 to 11
- tile_mask: int32 [128, 128, 128, 128], P('vert'), may hold values 0 or 1
- tile_count: int32 [128], P('vert'), may hold values from 32 to 128, as said below
- w_self1: bfloat16 [512, 512], replicated, may hold values from -0.25 to 0.25
- w_neigh1: bfloat16 [512, 512], replicated, may hold values from -1 to 1
- bias1: bfloat16 [512], replicated, may hold values from -3 to 3
- w_self2: bfloat16 [512, 512], replicated, may hold values from -0.25 to 0.25
- w_neigh2: bfloat16 [512, 512], replicated, may hold values from -1 to 1
- bias2: bfloat16 [512], replicated, may hold values from -3 to 3
Outputs:
- embedding: bfloat16 [131072, 512], P('vert')
The draws below stay inside these ranges and needn't reach their ends.
Inputs may be any that keep to these rules, and one draw needn't show every extreme that they name: `mirror_count`: some device has all 4 slots live on every peer, and some device receives 4 live rows from every device. `tile_count`: some device has all 128 tiles live.
All inputs are finite; a program needn't handle non-finite values. No bound on the sum of `tile_mask` on one device may be relied on, other than what follows from the above.
Results may differ from the reference program's by a relative error of at most 0.0051.
Values may be sent and summed in bfloat16 or wider, within the bound.
No kernel may reach another device: no remote copies, remote signals or barrier semaphores. Data moves between devices by JAX's collectives and lax.ppermute only.
A program may use at most 128 MiB of HBM per device.

```python
import math
import jax
import jax.numpy as jnp
import numpy as np
from jax import lax

F = 512
TB = 128
NODE_DEV = 1024
MR = 4
TILES_DEV = 128
NODES = 131072
TBLK = 12
N_VERT = 128


def draw_mirror_count(key, part):
    first, second, third = jax.random.split(key, 3)
    base = jax.random.randint(first, (N_VERT, N_VERT), 1, MR + 1, dtype=jnp.int32)
    ranked = jax.random.permutation(second, N_VERT)
    hubs = ranked < max(N_VERT // 8, 1)
    column = jax.random.randint(third, (), 0, N_VERT, dtype=jnp.int32)
    filled = jnp.where(hubs[:, None], MR, base)
    return jnp.where(jnp.arange(N_VERT, dtype=jnp.int32)[None, :] == column, MR, filled).astype(jnp.int32)


def draw_tile_count(key, part):
    first, second = jax.random.split(key, 2)
    base = jax.random.randint(first, (N_VERT,), TILES_DEV // 4, TILES_DEV + 1, dtype=jnp.int32)
    busiest = jax.random.randint(second, (), 0, N_VERT, dtype=jnp.int32)
    return jnp.where(jnp.arange(N_VERT, dtype=jnp.int32) == busiest, TILES_DEV, base).astype(jnp.int32)


def place_ends(entries, own_key, least, top_value):
    index_at = [jax.random.randint(jax.random.fold_in(own_key, axis), (), 0, length) for axis, length in enumerate(entries.shape)]
    longest = entries.shape.index(max(entries.shape))
    next_to = index_at[:longest] + [(index_at[longest] + 1) % entries.shape[longest]] + index_at[longest + 1:]
    return entries.at[tuple(index_at)].set(least).at[tuple(next_to)].set(top_value)


def block_levels(key, dims, pieces, least, largest):
    factor_of = 1.0
    for axis_at, blocks in pieces:
        draws = jax.random.uniform(jax.random.fold_in(jax.random.fold_in(key, 6), axis_at), (blocks,), jnp.float32, least / len(pieces), largest / len(pieces))
        factor_of = factor_of * jnp.repeat(jnp.exp(draws), dims[axis_at] // blocks).reshape((-1,) + (1,) * (len(dims) - 1 - axis_at))
    return factor_of


def rank_bounds(amount, skew):
    loads = [(1 << 20) // math.isqrt(grade ** skew) + 1 for grade in range(1, amount + 1)]
    scale = 1 + sum(loads) // (1 << 30)
    return np.cumsum(np.array([max(1, weight // scale) for weight in loads]))


def skewed_ids(own_key, dims, amount, lean):
    grid = rank_bounds(amount, lean)
    pick = jax.random.randint(jax.random.fold_in(own_key, 1), dims, 0, int(grid[amount - 1]))
    grade = jnp.searchsorted(jnp.asarray(grid, jnp.int32), pick, side="right")
    return jax.random.permutation(jax.random.fold_in(own_key, 2), amount)[grade].astype(jnp.int32)


def bell_draw(own_key, extent, deviation, bound, pieces=(), kind=jnp.bfloat16):
    entries = deviation * jax.random.normal(own_key, extent, jnp.float32)
    if pieces:
        entries = entries * block_levels(own_key, extent, pieces, -0.22, 0.18)
    return jnp.clip(entries, -bound, bound).astype(kind)


def setup_inputs(seed: int = 0) -> dict:
    splits = jax.random.split(jax.random.key(seed), 13)
    features = bell_draw(splits[0], (NODES, F), 1.0, 6.0, ((0, 128),))
    send_rows = place_ends(skewed_ids(splits[1], (N_VERT, N_VERT, MR), NODE_DEV, 2), jax.random.fold_in(splits[1], 3), 0, NODE_DEV - 1).astype(jnp.int32)
    mirror_count = draw_mirror_count(jax.random.fold_in(splits[12], 71), 0)
    tile_coord = place_ends(jax.random.randint(splits[3], (N_VERT, 2, TILES_DEV), 0, TBLK), jax.random.fold_in(splits[3], 1), 0, TBLK - 1).astype(jnp.int32)
    tile_mask = place_ends((jax.random.randint(splits[4], (N_VERT, TILES_DEV, TB, TB), 0, 8) < 1).astype(jnp.int32), jax.random.fold_in(splits[4], 1), 0, 1)
    tile_count = draw_tile_count(jax.random.fold_in(splits[12], 71), 0)
    w_self1 = bell_draw(splits[6], (F, F), F ** -0.5, 0.25)
    w_neigh1 = bell_draw(splits[7], (F, F), (F // 16) ** -0.5, 1.0)
    bias1 = bell_draw(splits[8], (F,), 0.5, 3.0)
    w_self2 = bell_draw(splits[9], (F, F), F ** -0.5, 0.25)
    w_neigh2 = bell_draw(splits[10], (F, F), (F // 16) ** -0.5, 1.0)
    bias2 = bell_draw(splits[11], (F,), 0.5, 3.0)
    return dict(features=features, send_rows=send_rows, mirror_count=mirror_count, tile_coord=tile_coord, tile_mask=tile_mask, tile_count=tile_count, w_self1=w_self1, w_neigh1=w_neigh1, bias1=bias1, w_self2=w_self2, w_neigh2=w_neigh2, bias2=bias2)


def reference(features, send_rows, mirror_count, tile_coord, tile_mask, tile_count, w_self1, w_neigh1, bias1, w_self2, w_neigh2, bias2):
    nodes, width = features.shape
    number = send_rows.shape[0]
    own_rows = nodes // number
    slots = send_rows.shape[2]
    block = tile_mask.shape[2]
    tiles = tile_mask.shape[1]
    peers = jnp.arange(number, dtype=jnp.int32)

    def layout(device):
        mirror_ids = peers[:, None] * own_rows + send_rows[:, device, :].astype(jnp.int32)
        mirror_live = jnp.arange(slots, dtype=jnp.int32)[None, :] < mirror_count[:, device][:, None]
        ids = jnp.concatenate([device * own_rows + jnp.arange(own_rows, dtype=jnp.int32), mirror_ids.reshape(-1)])
        alive = jnp.concatenate([jnp.ones((own_rows,), bool), mirror_live.reshape(-1)])
        return ids.astype(jnp.int32), alive

    def aggregate(current):
        values = current.astype(jnp.float32)

        def visit(carry, device):
            totals, degree = carry
            ids, alive = layout(device)
            table = values[ids].reshape(-1, block, width)
            live_source = alive.astype(jnp.float32).reshape(-1, block)
            used = (jnp.arange(tiles, dtype=jnp.int32) < tile_count[device]).astype(jnp.float32)
            target = tile_coord[device, 0]
            source = tile_coord[device, 1]
            weights = tile_mask[device].astype(jnp.float32) * used[:, None, None] * live_source[source][:, None, :]
            products = jnp.einsum("tij,tjf->tif", weights, table[source], precision=lax.Precision.HIGHEST)
            local = jnp.zeros(table.shape, jnp.float32).at[target].add(products).reshape(-1, width)
            counted = jnp.zeros(live_source.shape, jnp.float32).at[target].add(jnp.sum(weights, axis=2)).reshape(-1)
            keep = alive.astype(jnp.float32)
            totals = totals.at[ids].add(local * keep[:, None])
            degree = degree.at[ids].add(counted * keep)
            return (totals, degree), None

        start = (jnp.zeros((nodes, width), jnp.float32), jnp.zeros((nodes,), jnp.float32))
        (totals, degree), _ = lax.scan(visit, start, peers)
        return totals, degree

    current = features
    for layer, (w_self, w_neigh, bias) in enumerate(((w_self1, w_neigh1, bias1), (w_self2, w_neigh2, bias2))):
        summed, degree = aggregate(current)
        mean = ((summed + current.astype(jnp.float32)) / (degree + 1.0)[:, None]).astype(jnp.bfloat16)
        pre = jnp.dot(current, w_self, preferred_element_type=jnp.float32) + jnp.dot(mean, w_neigh, preferred_element_type=jnp.float32) + bias.astype(jnp.float32)
        if layer == 0:
            current = jax.nn.relu(pre).astype(jnp.bfloat16)
        else:
            current = pre.astype(jnp.bfloat16)
    return current
```

```python
import jax
import jax.numpy as jnp
from jax import lax
from jax.experimental import pallas as pl
from jax.experimental.pallas import tpu as pltpu
from jax.sharding import PartitionSpec as P

GROUP = 8
DEAD = 64.0
BF = jnp.bfloat16
F32 = jnp.float32


def dot(a, b):
    return jnp.dot(a, b, preferred_element_type=F32)


def low_half(pairs):
    return lax.broadcasted_iota(jnp.int32, (pairs, 8, 128), 1) < 4


def pack(columns, out_ref):
    pairs = out_ref.shape[0]
    low = low_half(pairs)
    for h in range(len(columns) // 2):
        first = columns[2 * h].reshape(pairs, 8, 128)
        second = columns[2 * h + 1].reshape(pairs, 8, 128)
        even = jnp.where(low, first, pltpu.roll(second, 4, 1))
        odd = jnp.where(low, pltpu.roll(first, 4, 1), second)
        out_ref[:, 0, h] = even.astype(BF)
        out_ref[:, 1, h] = odd.astype(BF)


def unpack(in_ref, h):
    pairs = in_ref.shape[0]
    low = low_half(pairs)
    even = in_ref[:, 0, h].astype(F32)
    odd = in_ref[:, 1, h].astype(F32)
    first = jnp.where(low, even, pltpu.roll(odd, 4, 1))
    second = jnp.where(low, pltpu.roll(even, 4, 1), odd)
    return first.reshape(pairs * 8, 128), second.reshape(pairs * 8, 128)


def lane_tiles(array):
    return [array[:, c * 128 : (c + 1) * 128] for c in range(array.shape[1] // 128)]


def first_gather(index_ref, x_ref, pick_ref, out_ref):
    index = index_ref[...]
    nodes = x_ref.shape[0]
    lane = lax.broadcasted_iota(jnp.int32, index.shape, 1)
    for j in range(nodes // 128):
        pick_ref[:, j * 128 : (j + 1) * 128] = (index == lane + j * 128).astype(F32).astype(BF)
    rows = dot(pick_ref[...], x_ref[...])
    dead = index >= nodes
    pack([jnp.where(dead, DEAD, tile) for tile in lane_tiles(rows)], out_ref)


def own_sources(adj_ref, x_ref, part_ref):
    own = x_ref.shape[0]
    for k in range(part_ref.shape[0] // 256):
        rows = slice(k * 256, (k + 1) * 256)
        part_ref[rows, :] = dot(adj_ref[rows, :own], x_ref[...])


def build_adjacency(coord_ref, count_ref, mask_ref, x_ref, adj_ref, part_ref, edges_ref):
    step = pl.program_id(0)
    live = count_ref[0]

    @pl.when(step == 0)
    def _():
        adj_ref[...] = jnp.zeros_like(adj_ref)

    for j in range(GROUP):
        tile = step * GROUP + j

        @pl.when(tile < live)
        def _(j=j, tile=tile):
            to = pl.ds(pl.multiple_of(coord_ref[0, tile] * 128, 128), 128)
            src = pl.ds(pl.multiple_of(coord_ref[1, tile] * 128, 128), 128)
            adj_ref[to, src] += mask_ref[j].astype(F32).astype(BF)

    @pl.when(step == pl.num_programs(0) - 1)
    def _():
        own_sources(adj_ref, x_ref, part_ref)
        own = x_ref.shape[0]
        ones = jnp.ones((own, 128), BF)
        for k in range(part_ref.shape[0] // 256):
            rows = slice(k * 256, (k + 1) * 256)
            edges_ref[rows, :] = dot(adj_ref[rows, :own], ones)


def mirror_sums_first(in_ref, adj_ref, part_ref, edges_ref, table_ref, live_ref, out_ref):
    for h in range(2):
        for c, tile in zip((2 * h, 2 * h + 1), unpack(in_ref, h)):
            dead = tile > DEAD / 2
            table_ref[:, c * 128 : (c + 1) * 128] = jnp.where(dead, 0.0, tile).astype(BF)
            if c == 0:
                live_ref[...] = jnp.where(dead, 0.0, 1.0).astype(BF)
    adj = adj_ref[...]
    sums = part_ref[...] + dot(adj, table_ref[...])
    edges = edges_ref[...] + dot(adj, live_ref[...])
    high = jnp.floor(edges * (1.0 / 128.0))
    pack(lane_tiles(sums) + [high, edges - 128.0 * high], out_ref)


def mirror_sums(in_ref, adj_ref, part_ref, table_ref, out_ref):
    for h in range(2):
        for c, tile in zip((2 * h, 2 * h + 1), unpack(in_ref, h)):
            table_ref[:, c * 128 : (c + 1) * 128] = tile.astype(BF)
    sums = part_ref[...] + dot(adj_ref[...], table_ref[...])
    pack(lane_tiles(sums), out_ref)


def own_sums_first(
    index_ref, adj_ref, part_ref, edges_ref, table_ref, live_ref, x_ref, w_ref, b_ref,
    sums_ref, count_ref, self_ref, place_ref,
):
    index = index_ref[...]
    for k in range(x_ref.shape[0] // 256):
        rows = slice(k * 256, (k + 1) * 256)
        adj = adj_ref[rows, :]
        x = x_ref[rows, :]
        sums_ref[rows, :] = part_ref[rows, :] + dot(adj, table_ref[...]) + x.astype(F32)
        count_ref[rows, :] = edges_ref[rows, :] + dot(adj, live_ref[...]) + 1.0
        self_ref[rows, :] = dot(x, w_ref[...]) + b_ref[...].astype(F32)
        row = lax.broadcasted_iota(jnp.int32, (256, index.shape[1]), 0) + k * 256
        place_ref[rows, :] = (row == index).astype(F32).astype(BF)


def own_sums(adj_ref, part_ref, table_ref, x_ref, sums_ref):
    for k in range(x_ref.shape[0] // 256):
        rows = slice(k * 256, (k + 1) * 256)
        sums_ref[rows, :] = (
            part_ref[rows, :] + dot(adj_ref[rows, :], table_ref[...]) + x_ref[rows, :].astype(F32)
        )


def scaled(sums, inverse):
    return jnp.concatenate([tile * inverse for tile in lane_tiles(sums)], axis=1).astype(BF)


def first_layer_end(
    in_ref, sums_ref, count_ref, self_ref, place_ref, pick_ref, w_ref,
    hidden_ref, inverse_ref, out_ref, back_ref,
):
    for h in range(3):
        for c, tile in zip((2 * h, 2 * h + 1), unpack(in_ref, h)):
            back_ref[:, c * 128 : (c + 1) * 128] = tile.astype(BF)
    for k in range(hidden_ref.shape[0] // 256):
        rows = slice(k * 256, (k + 1) * 256)
        returned = dot(place_ref[rows, :], back_ref[...])
        degree = count_ref[rows, :] + 128.0 * returned[:, 512:640] + returned[:, 640:]
        inverse = 1.0 / degree
        inverse_ref[rows, :] = inverse
        mean = scaled(sums_ref[rows, :] + returned[:, :512], inverse)
        pre = self_ref[rows, :] + dot(mean, w_ref[...])
        hidden_ref[rows, :] = jnp.maximum(pre, 0.0).astype(BF)
    pack(lane_tiles(dot(pick_ref[...], hidden_ref[...])), out_ref)


def second_own(adj_ref, x_ref, w_ref, b_ref, part_ref, self_ref):
    own_sources(adj_ref, x_ref, part_ref)
    for k in range(x_ref.shape[0] // 256):
        rows = slice(k * 256, (k + 1) * 256)
        self_ref[rows, :] = dot(x_ref[rows, :], w_ref[...]) + b_ref[...].astype(F32)


def second_layer_end(in_ref, sums_ref, inverse_ref, self_ref, place_ref, w_ref, out_ref, back_ref):
    for h in range(2):
        for c, tile in zip((2 * h, 2 * h + 1), unpack(in_ref, h)):
            back_ref[:, c * 128 : (c + 1) * 128] = tile.astype(BF)
    for k in range(out_ref.shape[0] // 256):
        rows = slice(k * 256, (k + 1) * 256)
        returned = dot(place_ref[rows, :], back_ref[...])
        mean = scaled(sums_ref[rows, :] + returned, inverse_ref[rows, :])
        out_ref[rows, :] = (self_ref[rows, :] + dot(mean, w_ref[...])).astype(BF)


def whole(shape):
    return pl.BlockSpec(shape, lambda *_: (0,) * len(shape))


def part_of(shape, *where):
    return pl.BlockSpec(shape, lambda *_: where)


def call(kernel, name, in_specs, outs, scratch=(), flops=0):
    return pl.pallas_call(
        kernel,
        name=name,
        grid=(1,),
        in_specs=in_specs,
        out_specs=[whole(o.shape) for o in outs],
        out_shape=list(outs),
        scratch_shapes=list(scratch),
        cost_estimate=pl.CostEstimate(flops=flops, bytes_accessed=1 << 20, transcendentals=0),
        compiler_params=pltpu.CompilerParams(vmem_limit_bytes=40 << 20),
    )


def array(*shape, dtype=F32):
    return jax.ShapeDtypeStruct(shape, dtype)


def exchange(packed):
    pairs, two, halves, eight, lanes = packed.shape
    sent = packed.reshape(pairs * two, halves * eight, lanes)
    arrived = lax.all_to_all(sent, "vert", split_axis=0, concat_axis=0, tiled=True)
    return arrived.reshape(packed.shape)


def body(
    features, send_rows, mirror_count, tile_coord, tile_mask, tile_count,
    w_self1, w_neigh1, bias1, w_self2, w_neigh2, bias2,
):
    own, width = features.shape
    _, peers, slots = send_rows.shape
    block = tile_mask.shape[2]
    tiles = tile_mask.shape[1]
    mirrors = peers * slots
    rows = own + mirrors
    pairs = peers // 2
    message = (pairs, 2, 2, 8, 128)
    longer = (pairs, 2, 3, 8, 128)

    live_slot = jnp.arange(slots, dtype=jnp.int32)[None, :] < mirror_count[0][:, None]
    index = jnp.where(live_slot, send_rows[0], 2 * own)
    index_row = index.reshape(1, mirrors)
    index_column = jnp.broadcast_to(index.reshape(mirrors, 1), (mirrors, 128))

    pick, sent = call(
        first_gather, "first_gather",
        [whole((mirrors, 128)), whole((own, width))],
        [array(mirrors, own, dtype=BF), array(*message, dtype=BF)],
        flops=2 * mirrors * own * width,
    )(index_column, features)
    arrived = exchange(sent)

    adj, part, edges = pl.pallas_call(
        build_adjacency,
        name="build_adjacency",
        grid_spec=pltpu.PrefetchScalarGridSpec(
            num_scalar_prefetch=2,
            grid=(tiles // GROUP,),
            in_specs=[
                pl.BlockSpec(
                    (GROUP, block, block),
                    lambda i, coord, count: (
                        jnp.minimum(i, jnp.maximum(count[0] - 1, 0) // GROUP), 0, 0,
                    ),
                ),
                whole((own, width)),
            ],
            out_specs=[whole((rows, rows)), whole((rows, width)), whole((rows, 128))],
        ),
        out_shape=[array(rows, rows, dtype=BF), array(rows, width), array(rows, 128)],
        cost_estimate=pl.CostEstimate(
            flops=2 * rows * own * width, bytes_accessed=8 << 20, transcendentals=0
        ),
        compiler_params=pltpu.CompilerParams(vmem_limit_bytes=40 << 20),
    )(tile_coord[0], tile_count, tile_mask[0], features)

    adj_mirrors = part_of((mirrors, mirrors), own // mirrors, own // mirrors)
    adj_own = part_of((own, mirrors), 0, own // mirrors)
    table, live, sent = call(
        mirror_sums_first, "mirror_sums_first",
        [
            whole(message), adj_mirrors,
            part_of((mirrors, width), own // mirrors, 0),
            part_of((mirrors, 128), own // mirrors, 0),
        ],
        [array(mirrors, width, dtype=BF), array(mirrors, 128, dtype=BF), array(*longer, dtype=BF)],
        flops=2 * mirrors * mirrors * width,
    )(arrived, adj, part, edges)
    arrived = exchange(sent)

    sums, count, own_term, place = call(
        own_sums_first, "own_sums_first",
        [
            whole((1, mirrors)), adj_own, part_of((own, width), 0, 0), part_of((own, 128), 0, 0),
            whole((mirrors, width)), whole((mirrors, 128)), whole((own, width)),
            whole((width, width)), whole((1, width)),
        ],
        [array(own, width), array(own, 128), array(own, width), array(own, mirrors, dtype=BF)],
        flops=4 * own * mirrors * width,
    )(index_row, adj, part, edges, table, live, features, w_self1, bias1.reshape(1, width))

    hidden, inverse, sent = call(
        first_layer_end, "first_layer_end",
        [
            whole(longer), whole((own, width)), whole((own, 128)), whole((own, width)),
            whole((own, mirrors)), whole((mirrors, own)), whole((width, width)),
        ],
        [array(own, width, dtype=BF), array(own, 128), array(*message, dtype=BF)],
        [pltpu.VMEM((mirrors, width + 256), BF)],
        flops=6 * own * mirrors * width,
    )(arrived, sums, count, own_term, place, pick, w_neigh1)
    arrived = exchange(sent)

    part, own_term = call(
        second_own, "second_own",
        [part_of((rows, own), 0, 0), whole((own, width)), whole((width, width)), whole((1, width))],
        [array(rows, width), array(own, width)],
        flops=2 * rows * own * width,
    )(adj, hidden, w_self2, bias2.reshape(1, width))

    table, sent = call(
        mirror_sums, "mirror_sums",
        [whole(message), adj_mirrors, part_of((mirrors, width), own // mirrors, 0)],
        [array(mirrors, width, dtype=BF), array(*message, dtype=BF)],
        flops=2 * mirrors * mirrors * width,
    )(arrived, adj, part)
    arrived = exchange(sent)

    (sums,) = call(
        own_sums, "own_sums",
        [adj_own, part_of((own, width), 0, 0), whole((mirrors, width)), whole((own, width))],
        [array(own, width)],
        flops=2 * own * mirrors * width,
    )(adj, part, table, hidden)

    (embedding,) = call(
        second_layer_end, "second_layer_end",
        [
            whole(message), whole((own, width)), whole((own, 128)), whole((own, width)),
            whole((own, mirrors)), whole((width, width)),
        ],
        [array(own, width, dtype=BF)],
        [pltpu.VMEM((mirrors, width), BF)],
        flops=4 * own * mirrors * width,
    )(arrived, sums, inverse, own_term, place, w_neigh2)
    return embedding


def solution(mesh):
    in_specs = (
        P("vert", None),
        P("vert", None, None),
        P("vert", None),
        P("vert", None, None),
        P("vert", None, None, None),
        P("vert"),
        P(),
        P(),
        P(),
        P(),
        P(),
        P(),
    )
    out_specs = P("vert", None)
    return jax.shard_map(body, mesh=mesh, in_specs=in_specs, out_specs=out_specs, check_vma=False)
```

```python
import jax
import jax.numpy as jnp
from jax import lax
from jax.experimental import pallas as pl
from jax.experimental.pallas import tpu as pltpu
from jax.sharding import PartitionSpec as P

GROUP = 8
STEP = 256
DEAD = 64.0
LIMIT = 63_400_000
BF = jnp.bfloat16
F32 = jnp.float32
HBM = pl.BlockSpec(memory_space=pltpu.HBM)


def dot(a, b):
    return jnp.dot(a, b, preferred_element_type=F32)


def iota(shape, axis):
    return lax.broadcasted_iota(jnp.int32, shape, axis)


def start(src, dst, sem):
    copy = pltpu.make_async_copy(src, dst, sem)
    copy.start()
    return copy


def finish(copies):
    for copy in copies:
        copy.wait()


def chunks(rows):
    return [slice(k, k + STEP) for k in range(0, rows, STEP)]


def pack(columns, out_ref, pair):
    pairs = columns[0].shape[0] // 8
    low = iota((pairs, 8, 128), 1) < 4
    for h in range(len(columns) // 2):
        first = columns[2 * h].reshape(pairs, 8, 128)
        second = columns[2 * h + 1].reshape(pairs, 8, 128)
        even = jnp.where(low, first, pltpu.roll(second, 4, 1))
        odd = jnp.where(low, pltpu.roll(first, 4, 1), second)
        out_ref[pair : pair + pairs, 0, h] = even.astype(BF)
        out_ref[pair : pair + pairs, 1, h] = odd.astype(BF)


def unpack(in_ref, h):
    pairs = in_ref.shape[0]
    low = iota((pairs, 8, 128), 1) < 4
    even = in_ref[:, 0, h].astype(F32)
    odd = in_ref[:, 1, h].astype(F32)
    first = jnp.where(low, even, pltpu.roll(odd, 4, 1))
    second = jnp.where(low, pltpu.roll(even, 4, 1), odd)
    return first.reshape(pairs * 8, 128), second.reshape(pairs * 8, 128)


def unpack_into(in_ref, table_ref):
    for h in range(in_ref.shape[2]):
        for c, tile in zip((2 * h, 2 * h + 1), unpack(in_ref, h)):
            table_ref[:, c * 128 : (c + 1) * 128] = tile.astype(BF)


def lane_tiles(array):
    return [array[:, c * 128 : (c + 1) * 128] for c in range(array.shape[1] // 128)]


def slot_rows(rows_ref, count_ref, never):
    slots, peers = rows_ref.shape
    live = iota((slots, peers), 0) < count_ref[...]
    value = jnp.where(live, rows_ref[...], never).astype(F32)
    value = jnp.concatenate([value, value], axis=0)
    shape = (peers // 2, 2 * slots, peers)
    row = iota(shape, 0) * 2 * slots + iota(shape, 1)
    mine = row // slots == iota(shape, 2)
    picked = jnp.where(mine, value[None], 0.0).reshape(peers * slots, peers)
    return jnp.sum(picked, axis=1, keepdims=True)


def fill_pick(slot, pick_ref):
    for j in range(pick_ref.shape[1] // 128):
        node = (iota((pick_ref.shape[0], 128), 1) + j * 128).astype(F32)
        pick_ref[:, j * 128 : (j + 1) * 128] = jnp.where(slot == node, 1.0, 0.0).astype(BF)


def first_gather(rows_hbm, count_hbm, x_hbm, out_hbm, rows, count, x, pick, out, sems):
    small = [start(rows_hbm, rows, sems.at[0]), start(count_hbm, count, sems.at[1])]
    features = start(x_hbm, x, sems.at[2])
    finish(small)
    nodes = x.shape[0]
    slot = slot_rows(rows, count, 2 * nodes)
    fill_pick(slot, pick)
    features.wait()
    done = []
    for k, part in enumerate(chunks(pick.shape[0])):
        picked = dot(pick[part, :], x[...])
        dead = slot[part] >= nodes
        pair = part.start // 8
        pack([jnp.where(dead, DEAD, tile) for tile in lane_tiles(picked)], out, pair)
        here = pl.ds(pair, STEP // 8)
        done.append(start(out.at[here], out_hbm.at[here], sems.at[3 + k]))
    finish(done)


def build_adjacency(
    coord, count, mask_hbm, x_hbm, adj_hbm, part_hbm, edges_hbm,
    mask, x, adj, part, edges, mask_sems, sems,
):
    live = count[0]
    groups = (live + GROUP - 1) // GROUP

    def group_copy(g):
        here = pl.ds(g * GROUP, GROUP)
        return pltpu.make_async_copy(mask_hbm.at[here], mask.at[here], mask_sems.at[g])

    lax.fori_loop(0, groups, lambda g, c: (group_copy(g).start(), c)[1], 0)
    features = start(x_hbm, x, sems.at[0])
    adj[...] = jnp.zeros_like(adj)

    def add_group(g, carry):
        group_copy(g).wait()
        for j in range(GROUP):
            tile = g * GROUP + j

            @pl.when(tile < live)
            def _(tile=tile):
                to = pl.ds(pl.multiple_of(coord[0, tile] * 128, 128), 128)
                src = pl.ds(pl.multiple_of(coord[1, tile] * 128, 128), 128)
                adj[to, src] += mask[tile].astype(F32).astype(BF)

        return carry

    lax.fori_loop(0, groups, add_group, 0)
    done = [start(adj, adj_hbm, sems.at[1])]
    features.wait()
    own = x.shape[0]
    ones = jnp.ones((own, 128), BF)
    for k, rows in enumerate(chunks(part.shape[0])):
        source = adj[own + rows.start : own + rows.stop, :own]
        part[rows, :] = dot(source, x[...])
        edges[rows, :] = dot(source, ones)
    done += [start(part, part_hbm, sems.at[2]), start(edges, edges_hbm, sems.at[3])]
    finish(done)


def mirror_first(
    in_hbm, adj_hbm, part_hbm, edges_hbm, table_hbm, live_hbm, out_hbm,
    packed, adj, part, edges, table, live, out, sems,
):
    arrived = start(in_hbm, packed, sems.at[0])
    size = adj.shape[0]
    own = adj_hbm.shape[0] - size
    weights = start(adj_hbm.at[pl.ds(own, size), pl.ds(own, size)], adj, sems.at[1])
    rest = [start(part_hbm, part, sems.at[2]), start(edges_hbm, edges, sems.at[3])]
    arrived.wait()
    for h in range(packed.shape[2]):
        for c, tile in zip((2 * h, 2 * h + 1), unpack(packed, h)):
            dead = tile > DEAD / 2
            table[:, c * 128 : (c + 1) * 128] = jnp.where(dead, 0.0, tile).astype(BF)
            if c == 0:
                live[...] = jnp.where(dead, 0.0, 1.0).astype(BF)
    done = [start(table, table_hbm, sems.at[4]), start(live, live_hbm, sems.at[5])]
    weights.wait()
    finish(rest)
    for k, rows in enumerate(chunks(size)):
        sums = part[rows, :] + dot(adj[rows, :], table[...])
        total = edges[rows, :] + dot(adj[rows, :], live[...])
        high = jnp.floor(total * (1.0 / 128.0))
        pair = rows.start // 8
        pack(lane_tiles(sums) + [high, total - 128.0 * high], out, pair)
        here = pl.ds(pair, STEP // 8)
        done.append(start(out.at[here], out_hbm.at[here], sems.at[6 + k]))
    finish(done)


def mirror_second(in_hbm, adj_hbm, part_hbm, table_hbm, out_hbm, packed, adj, part, table, out, sems):
    arrived = start(in_hbm, packed, sems.at[0])
    size = adj.shape[0]
    own = adj_hbm.shape[0] - size
    rest = [
        start(adj_hbm.at[pl.ds(own, size), pl.ds(own, size)], adj, sems.at[1]),
        start(part_hbm, part, sems.at[2]),
    ]
    arrived.wait()
    unpack_into(packed, table)
    done = [start(table, table_hbm, sems.at[3])]
    finish(rest)
    for k, rows in enumerate(chunks(size)):
        sums = part[rows, :] + dot(adj[rows, :], table[...])
        pair = rows.start // 8
        pack(lane_tiles(sums), out, pair)
        here = pl.ds(pair, STEP // 8)
        done.append(start(out.at[here], out_hbm.at[here], sems.at[4 + k]))
    finish(done)


def own_first(
    rows_hbm, count_hbm, adj_hbm, table_hbm, live_hbm, x_hbm, w_hbm, b_hbm,
    sums_hbm, degree_hbm, self_hbm, place_hbm, pick_hbm,
    rows_v, count_v, adj, table, live, x, w, b, sums, degree, own_term, place, pick, sems,
):
    nodes = x.shape[0]
    small = [start(rows_hbm, rows_v, sems.at[0]), start(count_hbm, count_v, sems.at[1])]
    loads = [
        start(adj_hbm.at[pl.ds(0, nodes)], adj, sems.at[2]),
        start(table_hbm, table, sems.at[3]),
        start(live_hbm, live, sems.at[4]),
        start(x_hbm, x, sems.at[5]),
        start(w_hbm, w, sems.at[6]),
        start(b_hbm, b, sems.at[7]),
    ]
    finish(small)
    slot = slot_rows(rows_v, count_v, 2 * nodes)
    fill_pick(slot, pick)
    done = [start(pick, pick_hbm, sems.at[8])]
    same = iota((128, 128), 0) == iota((128, 128), 1)
    for j in range(place.shape[1] // 128):
        lanes = slice(j * 128, (j + 1) * 128)
        wanted = jnp.sum(jnp.where(same, slot[lanes], 0.0), axis=0, keepdims=True)
        node = iota((nodes, 128), 0).astype(F32)
        place[:, lanes] = jnp.where(node == wanted, 1.0, 0.0).astype(BF)
    done.append(start(place, place_hbm, sems.at[9]))
    finish(loads)
    ones = jnp.ones((nodes, 128), BF)
    for k, rows in enumerate(chunks(nodes)):
        sums[rows, :] = (
            dot(adj[rows, :nodes], x[...]) + dot(adj[rows, nodes:], table[...]) + x[rows, :].astype(F32)
        )
        degree[rows, :] = dot(adj[rows, :nodes], ones) + dot(adj[rows, nodes:], live[...]) + 1.0
        own_term[rows, :] = dot(x[rows, :], w[...]) + b[...]
    done += [
        start(sums, sums_hbm, sems.at[10]),
        start(degree, degree_hbm, sems.at[11]),
        start(own_term, self_hbm, sems.at[12]),
    ]
    finish(done)


def own_second(
    adj_hbm, table_hbm, x_hbm, w_hbm, b_hbm, sums_hbm, self_hbm,
    adj, table, x, w, b, sums, own_term, sems,
):
    nodes = x.shape[0]
    loads = [
        start(adj_hbm.at[pl.ds(0, nodes)], adj, sems.at[0]),
        start(table_hbm, table, sems.at[1]),
        start(x_hbm, x, sems.at[2]),
        start(w_hbm, w, sems.at[3]),
        start(b_hbm, b, sems.at[4]),
    ]
    finish(loads)
    for k, rows in enumerate(chunks(nodes)):
        sums[rows, :] = (
            dot(adj[rows, :nodes], x[...]) + dot(adj[rows, nodes:], table[...]) + x[rows, :].astype(F32)
        )
        own_term[rows, :] = dot(x[rows, :], w[...]) + b[...]
    finish([start(sums, sums_hbm, sems.at[5]), start(own_term, self_hbm, sems.at[6])])


def mirror_part(adj_hbm, x_hbm, part_hbm, adj, x, part, sems):
    size, own = adj.shape
    loads = [
        start(adj_hbm.at[pl.ds(own, size), pl.ds(0, own)], adj, sems.at[0]),
        start(x_hbm, x, sems.at[1]),
    ]
    finish(loads)
    for k, rows in enumerate(chunks(size)):
        part[rows, :] = dot(adj[rows, :], x[...])
    start(part, part_hbm, sems.at[2]).wait()


def scaled(sums, inverse):
    return jnp.concatenate([tile * inverse for tile in lane_tiles(sums)], axis=1).astype(BF)


def first_end(
    in_hbm, place_hbm, degree_hbm, sums_hbm, w_hbm, self_hbm, pick_hbm,
    hidden_hbm, inverse_hbm, out_hbm,
    packed, place, degree, sums, w, own_term, pick, hidden, inverse, back, out, sems,
):
    arrived = start(in_hbm, packed, sems.at[0])
    need = [
        start(place_hbm, place, sems.at[1]),
        start(degree_hbm, degree, sems.at[2]),
        start(sums_hbm, sums, sems.at[3]),
        start(w_hbm, w, sems.at[4]),
        start(self_hbm, own_term, sems.at[5]),
    ]
    picks = start(pick_hbm, pick, sems.at[6])
    arrived.wait()
    unpack_into(packed, back)
    finish(need)
    width = hidden.shape[1]
    for k, rows in enumerate(chunks(hidden.shape[0])):
        returned = dot(place[rows, :], back[...])
        total = degree[rows, :] + 128.0 * returned[:, width : width + 128] + returned[:, width + 128 :]
        scale = 1.0 / total
        inverse[rows, :] = scale
        mean = scaled(sums[rows, :] + returned[:, :width], scale)
        pre = own_term[rows, :] + dot(mean, w[...])
        hidden[rows, :] = jnp.maximum(pre, 0.0).astype(BF)
    done = [start(hidden, hidden_hbm, sems.at[7]), start(inverse, inverse_hbm, sems.at[8])]
    picks.wait()
    for k, rows in enumerate(chunks(pick.shape[0])):
        pair = rows.start // 8
        pack(lane_tiles(dot(pick[rows, :], hidden[...])), out, pair)
        here = pl.ds(pair, STEP // 8)
        done.append(start(out.at[here], out_hbm.at[here], sems.at[9 + k]))
    finish(done)


def second_end(
    in_hbm, place_hbm, inverse_hbm, sums_hbm, w_hbm, self_hbm, out_hbm,
    packed, place, inverse, sums, w, own_term, back, out, sems,
):
    arrived = start(in_hbm, packed, sems.at[0])
    need = [
        start(place_hbm, place, sems.at[1]),
        start(inverse_hbm, inverse, sems.at[2]),
        start(sums_hbm, sums, sems.at[3]),
        start(w_hbm, w, sems.at[4]),
        start(self_hbm, own_term, sems.at[5]),
    ]
    arrived.wait()
    unpack_into(packed, back)
    finish(need)
    done = []
    for k, rows in enumerate(chunks(out.shape[0])):
        returned = dot(place[rows, :], back[...])
        mean = scaled(sums[rows, :] + returned, inverse[rows, :])
        out[rows, :] = (own_term[rows, :] + dot(mean, w[...])).astype(BF)
        done.append(start(out.at[rows], out_hbm.at[rows], sems.at[6 + k]))
    finish(done)


def array(*shape, dtype=F32):
    return jax.ShapeDtypeStruct(shape, dtype)


def call(kernel, outs, buffers, sems, flops, in_specs=None):
    def run(*operands):
        return pl.pallas_call(
            kernel,
            name=kernel.__name__,
            in_specs=in_specs or [HBM] * len(operands),
            out_specs=[HBM] * len(outs),
            out_shape=list(outs),
            scratch_shapes=[pltpu.VMEM(b.shape, b.dtype) for b in buffers]
            + [pltpu.SemaphoreType.DMA((n,)) for n in sems],
            cost_estimate=pl.CostEstimate(flops=flops, bytes_accessed=4 << 20, transcendentals=0),
            compiler_params=pltpu.CompilerParams(vmem_limit_bytes=LIMIT),
        )(*operands)

    return run


def exchange(packed):
    pairs, two, halves, eight, lanes = packed.shape
    sent = packed.reshape(pairs * two, halves * eight, lanes)
    arrived = lax.all_to_all(sent, "vert", split_axis=0, concat_axis=0, tiled=True)
    return arrived.reshape(packed.shape)


def body(
    features, send_rows, mirror_count, tile_coord, tile_mask, tile_count,
    w_self1, w_neigh1, bias1, w_self2, w_neigh2, bias2,
):
    own, width = features.shape
    _, peers, slots = send_rows.shape
    block = tile_mask.shape[2]
    tiles = tile_mask.shape[1]
    mirrors = peers * slots
    rows = own + mirrors
    pairs = peers // 2
    message = array(pairs, 2, 2, 8, 128, dtype=BF)
    longer = array(pairs, 2, 3, 8, 128, dtype=BF)
    nodes = array(own, width, dtype=BF)
    wide = array(own, width)
    narrow = array(own, 128)
    weight = array(width, width, dtype=BF)
    bias = array(1, width)
    table_a = array(mirrors, width, dtype=BF)
    live_a = array(mirrors, 128, dtype=BF)
    part_a = array(mirrors, width)
    edges_a = array(mirrors, 128)
    adj_a = array(rows, rows, dtype=BF)
    adj_own = array(own, rows, dtype=BF)
    adj_mirror = array(mirrors, mirrors, dtype=BF)
    adj_to_mirror = array(mirrors, own, dtype=BF)
    pick_a = array(mirrors, own, dtype=BF)
    place_a = array(own, mirrors, dtype=BF)
    slot_a = array(slots, peers, dtype=jnp.int32)
    count_a = array(1, peers, dtype=jnp.int32)

    slot_table = send_rows[0].T
    bias1 = bias1.astype(F32).reshape(1, width)
    bias2 = bias2.astype(F32).reshape(1, width)

    (sent,) = call(
        first_gather, [message], [slot_a, count_a, nodes, pick_a, message], [5],
        2 * mirrors * own * width,
    )(slot_table, mirror_count, features)
    arrived = exchange(sent)

    smem = pl.BlockSpec(memory_space=pltpu.SMEM)
    adj, part, edges = call(
        build_adjacency, [adj_a, part_a, edges_a],
        [array(tiles, block, block, dtype=jnp.int32), nodes, adj_a, part_a, edges_a],
        [tiles // GROUP, 4], 4 * rows * own * width, [smem, smem, HBM, HBM],
    )(tile_coord[0], tile_count, tile_mask[0], features)

    table, live, sent = call(
        mirror_first, [table_a, live_a, longer],
        [message, adj_mirror, part_a, edges_a, table_a, live_a, longer], [8],
        2 * mirrors * mirrors * width,
    )(arrived, adj, part, edges)
    arrived = exchange(sent)

    sums, degree, own_term, place, pick = call(
        own_first, [wide, narrow, wide, place_a, pick_a],
        [
            slot_a, count_a, adj_own, table_a, live_a, nodes, weight, bias,
            wide, narrow, wide, place_a, pick_a,
        ],
        [13], 4 * own * rows * width,
    )(slot_table, mirror_count, adj, table, live, features, w_self1, bias1)

    hidden, inverse, sent = call(
        first_end, [nodes, narrow, message],
        [
            longer, place_a, narrow, wide, weight, wide, pick_a,
            nodes, narrow, array(mirrors, width + 256, dtype=BF), message,
        ],
        [11], 6 * own * mirrors * width,
    )(arrived, place, degree, sums, w_neigh1, own_term, pick)
    arrived = exchange(sent)

    (part,) = call(
        mirror_part, [part_a], [adj_to_mirror, nodes, part_a], [3], 2 * mirrors * own * width
    )(adj, hidden)

    table, sent = call(
        mirror_second, [table_a, message], [message, adj_mirror, part_a, table_a, message], [6],
        2 * mirrors * mirrors * width,
    )(arrived, adj, part)
    arrived = exchange(sent)

    sums, own_term = call(
        own_second, [wide, wide], [adj_own, table_a, nodes, weight, bias, wide, wide], [7],
        4 * own * rows * width,
    )(adj, table, hidden, w_self2, bias2)

    (embedding,) = call(
        second_end, [nodes],
        [message, place_a, narrow, wide, weight, wide, table_a, nodes], [10],
        4 * own * mirrors * width,
    )(arrived, place, inverse, sums, w_neigh2, own_term)
    return embedding


def solution(mesh):
    in_specs = (
        P("vert", None),
        P("vert", None, None),
        P("vert", None),
        P("vert", None, None),
        P("vert", None, None, None),
        P("vert"),
        P(),
        P(),
        P(),
        P(),
        P(),
        P(),
    )
    out_specs = P("vert", None)
    return jax.shard_map(body, mesh=mesh, in_specs=in_specs, out_specs=out_specs, check_vma=False)
```

```python
import jax
import jax.numpy as jnp
from jax import lax
from jax.experimental import pallas as pl
from jax.experimental.pallas import tpu as pltpu
from jax.sharding import PartitionSpec as P

GROUP = 8
STEP = 256
DEAD = 64.0
LIMIT = 55_000_000
BF = jnp.bfloat16
F32 = jnp.float32
HBM = pl.BlockSpec(memory_space=pltpu.HBM)
VMEM = pl.BlockSpec(memory_space=pltpu.VMEM)
SMEM = pl.BlockSpec(memory_space=pltpu.SMEM)


def dot(a, b):
    return jnp.dot(a, b, preferred_element_type=F32)


def iota(shape, axis):
    return lax.broadcasted_iota(jnp.int32, shape, axis)


def start(src, dst, sem):
    copy = pltpu.make_async_copy(src, dst, sem)
    copy.start()
    return copy


def finish(copies):
    for copy in copies:
        copy.wait()


def chunks(rows):
    return [slice(k, k + STEP) for k in range(0, rows, STEP)]


def pack(columns, out_ref, pair):
    pairs = columns[0].shape[0] // 8
    low = iota((pairs, 8, 128), 1) < 4
    for h in range(len(columns) // 2):
        first = columns[2 * h].reshape(pairs, 8, 128)
        second = columns[2 * h + 1].reshape(pairs, 8, 128)
        even = jnp.where(low, first, pltpu.roll(second, 4, 1))
        odd = jnp.where(low, pltpu.roll(first, 4, 1), second)
        out_ref[pair : pair + pairs, 0, h] = even.astype(BF)
        out_ref[pair : pair + pairs, 1, h] = odd.astype(BF)


def unpack(in_ref, h):
    pairs = in_ref.shape[0]
    low = iota((pairs, 8, 128), 1) < 4
    even = in_ref[:, 0, h].astype(F32)
    odd = in_ref[:, 1, h].astype(F32)
    first = jnp.where(low, even, pltpu.roll(odd, 4, 1))
    second = jnp.where(low, pltpu.roll(even, 4, 1), odd)
    return first.reshape(pairs * 8, 128), second.reshape(pairs * 8, 128)


def unpack_into(in_ref, table_ref):
    for h in range(in_ref.shape[2]):
        for c, tile in zip((2 * h, 2 * h + 1), unpack(in_ref, h)):
            table_ref[:, c * 128 : (c + 1) * 128] = tile.astype(BF)


def pack_fours(columns, out_ref, pair):
    pairs = columns[0].shape[0] // 8
    for c, column in enumerate(columns):
        both = column.reshape(pairs, 8, 128).astype(BF)
        out_ref[pair : pair + pairs, 0, c] = both[:, :4]
        out_ref[pair : pair + pairs, 1, c] = both[:, 4:]


def unpack_fours(in_ref, c):
    both = jnp.concatenate([in_ref[:, 0, c].astype(F32), in_ref[:, 1, c].astype(F32)], axis=1)
    return both.reshape(-1, 128)


def lane_tiles(array):
    return [array[:, c * 128 : (c + 1) * 128] for c in range(array.shape[1] // 128)]


def slot_rows(rows_ref, count_ref, never):
    slots, peers = rows_ref.shape
    live = iota((slots, peers), 0) < count_ref[...]
    value = jnp.where(live, rows_ref[...], never).astype(F32)
    value = jnp.concatenate([value, value], axis=0)
    shape = (peers // 2, 2 * slots, peers)
    row = iota(shape, 0) * 2 * slots + iota(shape, 1)
    mine = row // slots == iota(shape, 2)
    picked = jnp.where(mine, value[None], 0.0).reshape(peers * slots, peers)
    return jnp.sum(picked, axis=1, keepdims=True)


def fill_pick(slot, pick_ref):
    for j in range(pick_ref.shape[1] // 128):
        node = (iota((pick_ref.shape[0], 128), 1) + j * 128).astype(F32)
        pick_ref[:, j * 128 : (j + 1) * 128] = jnp.where(slot == node, 1.0, 0.0).astype(BF)


def first_gather(rows_hbm, count_hbm, x_hbm, out_hbm, rows, count, x, pick, out, sems):
    small = [start(rows_hbm, rows, sems.at[0]), start(count_hbm, count, sems.at[1])]
    features = start(x_hbm, x, sems.at[2])
    finish(small)
    nodes = x.shape[0]
    slot = slot_rows(rows, count, 2 * nodes)
    fill_pick(slot, pick)
    features.wait()
    done = []
    for k, part in enumerate(chunks(pick.shape[0])):
        picked = dot(pick[part, :], x[...])
        dead = slot[part] >= nodes
        pair = part.start // 8
        pack([jnp.where(dead, DEAD, tile) for tile in lane_tiles(picked)], out, pair)
        here = pl.ds(pair, STEP // 8)
        done.append(start(out.at[here], out_hbm.at[here], sems.at[3 + k]))
    finish(done)


def build_adjacency(
    coord, count, mask_hbm, x_hbm, adj_hbm, part_hbm, edges_hbm,
    mask, x, adj, part, edges, mask_sems, sems,
):
    live = count[0]
    groups = (live + GROUP - 1) // GROUP

    def group_copy(g):
        here = pl.ds(g * GROUP, GROUP)
        return pltpu.make_async_copy(mask_hbm.at[here], mask.at[here], mask_sems.at[g])

    lax.fori_loop(0, groups, lambda g, c: (group_copy(g).start(), c)[1], 0)
    features = start(x_hbm, x, sems.at[0])
    adj[...] = jnp.zeros_like(adj)

    def add_group(g, carry):
        group_copy(g).wait()
        for j in range(GROUP):
            tile = g * GROUP + j

            @pl.when(tile < live)
            def _(tile=tile):
                to = pl.ds(pl.multiple_of(coord[0, tile] * 128, 128), 128)
                src = pl.ds(pl.multiple_of(coord[1, tile] * 128, 128), 128)
                adj[to, src] += mask[tile].astype(F32).astype(BF)

        return carry

    lax.fori_loop(0, groups, add_group, 0)
    done = [start(adj, adj_hbm, sems.at[1])]
    features.wait()
    own = x.shape[0]
    ones = jnp.ones((own, 128), BF)
    for k, rows in enumerate(chunks(part.shape[0])):
        source = adj[own + rows.start : own + rows.stop, :own]
        part[rows, :] = dot(source, x[...])
        edges[rows, :] = dot(source, ones)
    done += [start(part, part_hbm, sems.at[2]), start(edges, edges_hbm, sems.at[3])]
    finish(done)


def mirror_first(
    packed, adj_hbm, part_hbm, edges_hbm, table_hbm, live_hbm, out_hbm,
    adj, part, edges, table, live, out, sems,
):
    size = adj.shape[0]
    own = adj_hbm.shape[0] - size
    weights = start(adj_hbm.at[pl.ds(own, size), pl.ds(own, size)], adj, sems.at[1])
    rest = [start(part_hbm, part, sems.at[2]), start(edges_hbm, edges, sems.at[3])]
    for h in range(packed.shape[2]):
        for c, tile in zip((2 * h, 2 * h + 1), unpack(packed, h)):
            dead = tile > DEAD / 2
            table[:, c * 128 : (c + 1) * 128] = jnp.where(dead, 0.0, tile).astype(BF)
            if c == 0:
                live[...] = jnp.where(dead, 0.0, 1.0).astype(BF)
    done = [start(table, table_hbm, sems.at[4]), start(live, live_hbm, sems.at[5])]
    weights.wait()
    finish(rest)
    for k, rows in enumerate(chunks(size)):
        sums = part[rows, :] + dot(adj[rows, :], table[...])
        total = edges[rows, :] + dot(adj[rows, :], live[...])
        high = jnp.floor(total * (1.0 / 128.0))
        pair = rows.start // 8
        low = iota(total.shape, 1) < 64
        pack_fours(lane_tiles(sums) + [jnp.where(low, high, total - 128.0 * high)], out, pair)
        here = pl.ds(pair, STEP // 8)
        done.append(start(out.at[here], out_hbm.at[here], sems.at[6 + k]))
    finish(done)


def mirror_second(packed, adj_hbm, part_hbm, table_hbm, out_hbm, adj, part, table, out, sems):
    size = adj.shape[0]
    own = adj_hbm.shape[0] - size
    rest = [
        start(adj_hbm.at[pl.ds(own, size), pl.ds(own, size)], adj, sems.at[1]),
        start(part_hbm, part, sems.at[2]),
    ]
    unpack_into(packed, table)
    done = [start(table, table_hbm, sems.at[3])]
    finish(rest)
    for k, rows in enumerate(chunks(size)):
        sums = part[rows, :] + dot(adj[rows, :], table[...])
        pair = rows.start // 8
        pack(lane_tiles(sums), out, pair)
        here = pl.ds(pair, STEP // 8)
        done.append(start(out.at[here], out_hbm.at[here], sems.at[4 + k]))
    finish(done)


def own_first(
    rows_hbm, count_hbm, adj_hbm, table_hbm, live_hbm, x_hbm, w_hbm, v_hbm, b_hbm,
    sums_hbm, degree_hbm, self_hbm, place_hbm, pick_hbm,
    rows_v, count_v, adj, table, live, x, w, v, b, sums, degree, own_term, place, pick, sems,
):
    nodes = x.shape[0]
    small = [start(rows_hbm, rows_v, sems.at[0]), start(count_hbm, count_v, sems.at[1])]
    loads = [
        start(adj_hbm.at[pl.ds(0, nodes)], adj, sems.at[2]),
        start(table_hbm, table, sems.at[3]),
        start(live_hbm, live, sems.at[4]),
        start(x_hbm, x, sems.at[5]),
        start(w_hbm, w, sems.at[6]),
        start(b_hbm, b, sems.at[7]),
        start(v_hbm, v, sems.at[13]),
    ]
    finish(small)
    slot = slot_rows(rows_v, count_v, 2 * nodes)
    fill_pick(slot, pick)
    done = [start(pick, pick_hbm, sems.at[8])]
    same = iota((128, 128), 0) == iota((128, 128), 1)
    for j in range(place.shape[1] // 128):
        lanes = slice(j * 128, (j + 1) * 128)
        wanted = jnp.sum(jnp.where(same, slot[lanes], 0.0), axis=0, keepdims=True)
        node = iota((nodes, 128), 0).astype(F32)
        place[:, lanes] = jnp.where(node == wanted, 1.0, 0.0).astype(BF)
    done.append(start(place, place_hbm, sems.at[9]))
    finish(loads)
    ones = jnp.ones((nodes, 128), BF)
    for k, rows in enumerate(chunks(nodes)):
        total = (
            dot(adj[rows, :nodes], x[...]) + dot(adj[rows, nodes:], table[...]) + x[rows, :].astype(F32)
        )
        sums[rows, :] = dot(total.astype(BF), v[...])
        degree[rows, :] = dot(adj[rows, :nodes], ones) + dot(adj[rows, nodes:], live[...]) + 1.0
        own_term[rows, :] = dot(x[rows, :], w[...]) + b[...]
    done += [
        start(sums, sums_hbm, sems.at[10]),
        start(degree, degree_hbm, sems.at[11]),
        start(own_term, self_hbm, sems.at[12]),
    ]
    finish(done)


def own_second(
    adj_hbm, table_hbm, x_hbm, inverse_hbm, w_hbm, v_hbm, b_hbm, self_hbm,
    adj, table, x, inverse, w, v, b, own_term, sems,
):
    nodes = x.shape[0]
    pairs = zip(
        (adj_hbm.at[pl.ds(0, nodes)], table_hbm, x_hbm, inverse_hbm, w_hbm, v_hbm, b_hbm),
        (adj, table, x, inverse, w, v, b),
    )
    finish([start(src, dst, sems.at[k]) for k, (src, dst) in enumerate(pairs)])
    done = []
    for k, rows in enumerate(chunks(nodes)):
        total = (
            dot(adj[rows, :nodes], x[...]) + dot(adj[rows, nodes:], table[...]) + x[rows, :].astype(F32)
        )
        mean = scaled(total, inverse[rows, :]).astype(BF)
        own_term[rows, :] = dot(x[rows, :], w[...]) + dot(mean, v[...]) + b[...]
        done.append(start(own_term.at[rows], self_hbm.at[rows], sems.at[7 + k]))
    finish(done)


def mirror_part(adj_hbm, x_hbm, part_hbm, adj, x, part, sems):
    size, own = adj.shape
    loads = [
        start(adj_hbm.at[pl.ds(own, size), pl.ds(0, own)], adj, sems.at[0]),
        start(x_hbm, x, sems.at[1]),
    ]
    finish(loads)
    for k, rows in enumerate(chunks(size)):
        part[rows, :] = dot(adj[rows, :], x[...])
    start(part, part_hbm, sems.at[2]).wait()


def scaled(sums, inverse):
    return jnp.concatenate([tile * inverse for tile in lane_tiles(sums)], axis=1)


def first_end(
    packed, place_hbm, degree_hbm, sums_hbm, w_hbm, self_hbm, pick_hbm,
    hidden_hbm, inverse_hbm, out_hbm,
    place, degree, sums, w, own_term, pick, hidden, inverse, back, mixed, out, sems, sum_sems, self_sems,
):
    weights = start(w_hbm, w, sems.at[0])
    need = [start(place_hbm, place, sems.at[1]), start(degree_hbm, degree, sems.at[2])]
    steps = chunks(hidden.shape[0])
    own = [
        [
            start(sums_hbm.at[rows], sums.at[rows], sum_sems.at[k]),
            start(self_hbm.at[rows], own_term.at[rows], self_sems.at[k]),
        ]
        for k, rows in enumerate(steps)
    ]
    picks = start(pick_hbm, pick, sems.at[3])
    width = hidden.shape[1]
    for c in range(width // 128):
        back[:, c * 128 : (c + 1) * 128] = unpack_fours(packed, c).astype(BF)
    mixed[:, width:] = unpack_fours(packed, width // 128).astype(BF)
    weights.wait()
    mixed[:, :width] = dot(back[...], w[...]).astype(BF)
    finish(need)
    for k, rows in enumerate(steps):
        returned = dot(place[rows, :], mixed[...])
        edges = returned[:, width:]
        other = pltpu.roll(edges, 64, 1)
        low = iota(edges.shape, 1) < 64
        edges = jnp.where(low, 128.0 * edges + other, edges + 128.0 * other)
        finish(own[k])
        scale = 1.0 / (degree[rows, :] + edges)
        inverse[rows, :] = scale
        pre = own_term[rows, :] + scaled(sums[rows, :] + returned[:, :width], scale)
        hidden[rows, :] = jnp.maximum(pre, 0.0).astype(BF)
    done = [start(hidden, hidden_hbm, sems.at[4]), start(inverse, inverse_hbm, sems.at[5])]
    picks.wait()
    for k, rows in enumerate(chunks(pick.shape[0])):
        pair = rows.start // 8
        pack(lane_tiles(dot(pick[rows, :], hidden[...])), out, pair)
        here = pl.ds(pair, STEP // 8)
        done.append(start(out.at[here], out_hbm.at[here], sems.at[6 + k]))
    finish(done)


def second_end(
    packed, place_hbm, inverse_hbm, w_hbm, self_hbm, out_hbm,
    place, inverse, w, own_term, back, mixed, out, sems, self_sems,
):
    weights = start(w_hbm, w, sems.at[0])
    need = [start(place_hbm, place, sems.at[1]), start(inverse_hbm, inverse, sems.at[2])]
    steps = chunks(out.shape[0])
    own = [start(self_hbm.at[rows], own_term.at[rows], self_sems.at[k]) for k, rows in enumerate(steps)]
    unpack_into(packed, back)
    weights.wait()
    mixed[...] = dot(back[...], w[...]).astype(BF)
    finish(need)
    done = []
    for k, rows in enumerate(steps):
        returned = scaled(dot(place[rows, :], mixed[...]), inverse[rows, :])
        own[k].wait()
        out[rows, :] = (own_term[rows, :] + returned).astype(BF)
        done.append(start(out.at[rows], out_hbm.at[rows], sems.at[3 + k]))
    finish(done)


def array(*shape, dtype=F32):
    return jax.ShapeDtypeStruct(shape, dtype)


def call(kernel, outs, buffers, sems, flops, *in_specs):
    def run(*operands):
        held = [x for x, spec in zip(operands, in_specs) if spec is VMEM]
        room = sum(x.size * x.dtype.itemsize for x in held)
        limit = LIMIT - room
        return pl.pallas_call(
            kernel,
            name=kernel.__name__,
            in_specs=list(in_specs) + [HBM] * (len(operands) - len(in_specs)),
            out_specs=[HBM] * len(outs),
            out_shape=list(outs),
            scratch_shapes=[pltpu.VMEM(b.shape, b.dtype) for b in buffers]
            + [pltpu.SemaphoreType.DMA((n,)) for n in sems],
            cost_estimate=pl.CostEstimate(flops=flops, bytes_accessed=4 << 20, transcendentals=0),
            compiler_params=pltpu.CompilerParams(vmem_limit_bytes=limit),
        )(*operands)

    return run


def exchange(packed):
    sent = packed.reshape((-1,) + packed.shape[2:])
    if packed.shape[3] == 8:
        sent = packed.reshape(sent.shape[0], -1, 128)
    arrived = lax.all_to_all(sent, "vert", split_axis=0, concat_axis=0, tiled=True)
    return arrived.reshape(packed.shape)


def body(
    features, send_rows, mirror_count, tile_coord, tile_mask, tile_count,
    w_self1, w_neigh1, bias1, w_self2, w_neigh2, bias2,
):
    own, width = features.shape
    _, peers, slots = send_rows.shape
    block = tile_mask.shape[2]
    tiles = tile_mask.shape[1]
    mirrors = peers * slots
    rows = own + mirrors
    pairs = peers // 2
    message = array(pairs, 2, 2, 8, 128, dtype=BF)
    longer = array(pairs, 2, 5, 4, 128, dtype=BF)
    nodes = array(own, width, dtype=BF)
    wide = array(own, width)
    narrow = array(own, 128)
    weight = array(width, width, dtype=BF)
    bias = array(1, width)
    table_a = array(mirrors, width, dtype=BF)
    live_a = array(mirrors, 128, dtype=BF)
    part_a = array(mirrors, width)
    edges_a = array(mirrors, 128)
    adj_a = array(rows, rows, dtype=BF)
    adj_own = array(own, rows, dtype=BF)
    adj_mirror = array(mirrors, mirrors, dtype=BF)
    adj_to_mirror = array(mirrors, own, dtype=BF)
    pick_a = array(mirrors, own, dtype=BF)
    place_a = array(own, mirrors, dtype=BF)
    slot_a = array(slots, peers, dtype=jnp.int32)
    count_a = array(1, peers, dtype=jnp.int32)

    slot_table = send_rows[0].T
    bias1 = bias1.astype(F32).reshape(1, width)
    bias2 = bias2.astype(F32).reshape(1, width)

    (sent,) = call(
        first_gather, [message], [slot_a, count_a, nodes, pick_a, message], [5],
        2 * mirrors * own * width,
    )(slot_table, mirror_count, features)
    arrived = exchange(sent)

    adj, part, edges = call(
        build_adjacency, [adj_a, part_a, edges_a],
        [array(tiles, block, block, dtype=jnp.int32), nodes, adj_a, part_a, edges_a],
        [tiles // GROUP, 4], 4 * rows * own * width, SMEM, SMEM,
    )(tile_coord[0], tile_count, tile_mask[0], features)

    table, live, sent = call(
        mirror_first, [table_a, live_a, longer],
        [adj_mirror, part_a, edges_a, table_a, live_a, longer], [8],
        2 * mirrors * mirrors * width, VMEM,
    )(arrived, adj, part, edges)
    arrived = exchange(sent)

    sums, degree, own_term, place, pick = call(
        own_first, [wide, narrow, wide, place_a, pick_a],
        [
            slot_a, count_a, adj_own, table_a, live_a, nodes, weight, weight, bias,
            wide, narrow, wide, place_a, pick_a,
        ],
        [14], 4 * own * rows * width,
    )(slot_table, mirror_count, adj, table, live, features, w_self1, w_neigh1, bias1)

    hidden, inverse, sent = call(
        first_end, [nodes, narrow, message],
        [
            place_a, narrow, wide, weight, wide, pick_a,
            nodes, narrow, table_a, array(mirrors, width + 128, dtype=BF), message,
        ],
        [8, own // STEP, own // STEP], 6 * own * mirrors * width, VMEM,
    )(arrived, place, degree, sums, w_neigh1, own_term, pick)
    arrived = exchange(sent)

    (part,) = call(
        mirror_part, [part_a], [adj_to_mirror, nodes, part_a], [3], 2 * mirrors * own * width
    )(adj, hidden)

    table, sent = call(
        mirror_second, [table_a, message], [adj_mirror, part_a, table_a, message], [6],
        2 * mirrors * mirrors * width, VMEM,
    )(arrived, adj, part)
    arrived = exchange(sent)

    (own_term,) = call(
        own_second, [wide],
        [adj_own, table_a, nodes, narrow, weight, weight, bias, wide], [7 + own // STEP],
        4 * own * rows * width,
    )(adj, table, hidden, inverse, w_self2, w_neigh2, bias2)

    (embedding,) = call(
        second_end, [nodes],
        [place_a, narrow, weight, wide, table_a, table_a, nodes], [3 + own // STEP, own // STEP],
        4 * own * mirrors * width, VMEM,
    )(arrived, place, inverse, w_neigh2, own_term)
    return embedding


def solution(mesh):
    in_specs = (
        P("vert", None),
        P("vert", None, None),
        P("vert", None),
        P("vert", None, None),
        P("vert", None, None, None),
        P("vert"),
        P(),
        P(),
        P(),
        P(),
        P(),
        P(),
    )
    out_specs = P("vert", None)
    return jax.shard_map(body, mesh=mesh, in_specs=in_specs, out_specs=out_specs, check_vma=False)
```

```python
import jax
import jax.numpy as jnp
from jax import lax
from jax.experimental import pallas as pl
from jax.experimental.pallas import tpu as pltpu
from jax.sharding import PartitionSpec as P

GROUP = 8
STEP = 256
DEAD = 64.0
LIMIT = 55_000_000
ALL = 63_400_000
BF = jnp.bfloat16
F32 = jnp.float32
HBM = pl.BlockSpec(memory_space=pltpu.HBM)
VMEM = pl.BlockSpec(memory_space=pltpu.VMEM)
SMEM = pl.BlockSpec(memory_space=pltpu.SMEM)


def dot(a, b):
    return jnp.dot(a, b, preferred_element_type=F32)


def iota(shape, axis):
    return lax.broadcasted_iota(jnp.int32, shape, axis)


def start(src, dst, sem):
    copy = pltpu.make_async_copy(src, dst, sem)
    copy.start()
    return copy


def finish(copies):
    for copy in copies:
        copy.wait()


def chunks(rows):
    return [slice(k, k + STEP) for k in range(0, rows, STEP)]


def pack(columns, out_ref, pair):
    pairs = columns[0].shape[0] // 8
    low = iota((pairs, 8, 128), 1) < 4
    for h in range(len(columns) // 2):
        first = columns[2 * h].reshape(pairs, 8, 128)
        second = columns[2 * h + 1].reshape(pairs, 8, 128)
        even = jnp.where(low, first, pltpu.roll(second, 4, 1))
        odd = jnp.where(low, pltpu.roll(first, 4, 1), second)
        out_ref[pair : pair + pairs, 0, h] = even.astype(BF)
        out_ref[pair : pair + pairs, 1, h] = odd.astype(BF)


def unpack(in_ref, h):
    pairs = in_ref.shape[0]
    low = iota((pairs, 8, 128), 1) < 4
    even = in_ref[:, 0, h].astype(F32)
    odd = in_ref[:, 1, h].astype(F32)
    first = jnp.where(low, even, pltpu.roll(odd, 4, 1))
    second = jnp.where(low, pltpu.roll(even, 4, 1), odd)
    return first.reshape(pairs * 8, 128), second.reshape(pairs * 8, 128)


def unpack_into(in_ref, table_ref):
    for h in range(in_ref.shape[2]):
        for c, tile in zip((2 * h, 2 * h + 1), unpack(in_ref, h)):
            table_ref[:, c * 128 : (c + 1) * 128] = tile.astype(BF)


def pack_fours(columns, out_ref, pair):
    pairs = columns[0].shape[0] // 8
    for c, column in enumerate(columns):
        both = column.reshape(pairs, 8, 128).astype(BF)
        out_ref[pair : pair + pairs, 0, c] = both[:, :4]
        out_ref[pair : pair + pairs, 1, c] = both[:, 4:]


def unpack_fours(in_ref, c):
    both = jnp.concatenate([in_ref[:, 0, c].astype(F32), in_ref[:, 1, c].astype(F32)], axis=1)
    return both.reshape(-1, 128)


def lane_tiles(array):
    return [array[:, c * 128 : (c + 1) * 128] for c in range(array.shape[1] // 128)]


def slot_rows(rows_ref, count_ref, never):
    slots, peers = rows_ref.shape
    live = iota((slots, peers), 0) < count_ref[...]
    value = jnp.where(live, rows_ref[...], never).astype(F32)
    value = jnp.concatenate([value, value], axis=0)
    shape = (peers // 2, 2 * slots, peers)
    row = iota(shape, 0) * 2 * slots + iota(shape, 1)
    mine = row // slots == iota(shape, 2)
    picked = jnp.where(mine, value[None], 0.0).reshape(peers * slots, peers)
    return jnp.sum(picked, axis=1, keepdims=True)


def fill_pick(slot, pick_ref):
    for j in range(pick_ref.shape[1] // 128):
        node = (iota((pick_ref.shape[0], 128), 1) + j * 128).astype(F32)
        pick_ref[:, j * 128 : (j + 1) * 128] = jnp.where(slot == node, 1.0, 0.0).astype(BF)


def first_gather(rows_hbm, count_hbm, x_hbm, out_hbm, rows, count, x, pick, out, sems):
    small = [start(rows_hbm, rows, sems.at[0]), start(count_hbm, count, sems.at[1])]
    features = start(x_hbm, x, sems.at[2])
    finish(small)
    nodes = x.shape[0]
    slot = slot_rows(rows, count, 2 * nodes)
    fill_pick(slot, pick)
    features.wait()
    done = []
    for k, part in enumerate(chunks(pick.shape[0])):
        picked = dot(pick[part, :], x[...])
        dead = slot[part] >= nodes
        pair = part.start // 8
        pack([jnp.where(dead, DEAD, tile) for tile in lane_tiles(picked)], out, pair)
        here = pl.ds(pair, STEP // 8)
        done.append(start(out.at[here], out_hbm.at[here], sems.at[3 + k]))
    finish(done)


def build_adjacency(
    coord, count, mask_hbm, x_hbm, adj_hbm, part_hbm, edges_hbm,
    mask, x, adj, part, edges, mask_sems, sems,
):
    live = count[0]
    groups = (live + GROUP - 1) // GROUP

    def group_copy(g):
        here = pl.ds(g * GROUP, GROUP)
        return pltpu.make_async_copy(mask_hbm.at[here], mask.at[here], mask_sems.at[g])

    lax.fori_loop(0, groups, lambda g, c: (group_copy(g).start(), c)[1], 0)
    features = start(x_hbm, x, sems.at[0])
    adj[...] = jnp.zeros_like(adj)

    def add_group(g, carry):
        group_copy(g).wait()
        for j in range(GROUP):
            tile = g * GROUP + j

            @pl.when(tile < live)
            def _(tile=tile):
                to = pl.ds(pl.multiple_of(coord[0, tile] * 128, 128), 128)
                src = pl.ds(pl.multiple_of(coord[1, tile] * 128, 128), 128)
                adj[to, src] += mask[tile].astype(F32).astype(BF)

        return carry

    lax.fori_loop(0, groups, add_group, 0)
    done = [start(adj, adj_hbm, sems.at[1])]
    features.wait()
    own = x.shape[0]
    ones = jnp.ones((own, 128), BF)
    for k, rows in enumerate(chunks(part.shape[0])):
        source = adj[own + rows.start : own + rows.stop, :own]
        part[rows, :] = dot(source, x[...])
        edges[rows, :] = dot(source, ones)
    done += [start(part, part_hbm, sems.at[2]), start(edges, edges_hbm, sems.at[3])]
    finish(done)


def mirror_first(
    packed, adj_hbm, part_hbm, edges_hbm, table_hbm, live_hbm, out_hbm,
    adj, part, edges, table, live, out, sems,
):
    size = adj.shape[0]
    own = adj_hbm.shape[0] - size
    weights = start(adj_hbm.at[pl.ds(own, size), pl.ds(own, size)], adj, sems.at[1])
    rest = [start(part_hbm, part, sems.at[2]), start(edges_hbm, edges, sems.at[3])]
    for h in range(packed.shape[2]):
        for c, tile in zip((2 * h, 2 * h + 1), unpack(packed, h)):
            dead = tile > DEAD / 2
            table[:, c * 128 : (c + 1) * 128] = jnp.where(dead, 0.0, tile).astype(BF)
            if c == 0:
                live[...] = jnp.where(dead, 0.0, 1.0).astype(BF)
    done = [start(table, table_hbm, sems.at[4]), start(live, live_hbm, sems.at[5])]
    weights.wait()
    finish(rest)
    for k, rows in enumerate(chunks(size)):
        sums = part[rows, :] + dot(adj[rows, :], table[...])
        total = edges[rows, :] + dot(adj[rows, :], live[...])
        high = jnp.floor(total * (1.0 / 128.0))
        pair = rows.start // 8
        low = iota(total.shape, 1) < 64
        pack_fours(lane_tiles(sums) + [jnp.where(low, high, total - 128.0 * high)], out, pair)
        here = pl.ds(pair, STEP // 8)
        done.append(start(out.at[here], out_hbm.at[here], sems.at[6 + k]))
    finish(done)


def mirror_second(packed, adj_hbm, part_hbm, table_hbm, out_hbm, adj, part, table, out, sems):
    size = adj.shape[0]
    own = adj_hbm.shape[0] - size
    rest = [
        start(adj_hbm.at[pl.ds(own, size), pl.ds(own, size)], adj, sems.at[1]),
        start(part_hbm, part, sems.at[2]),
    ]
    unpack_into(packed, table)
    done = [start(table, table_hbm, sems.at[3])]
    finish(rest)
    for k, rows in enumerate(chunks(size)):
        sums = part[rows, :] + dot(adj[rows, :], table[...])
        pair = rows.start // 8
        pack(lane_tiles(sums), out, pair)
        here = pl.ds(pair, STEP // 8)
        done.append(start(out.at[here], out_hbm.at[here], sems.at[4 + k]))
    finish(done)


def own_first(
    rows_hbm, count_hbm, adj_hbm, table_hbm, live_hbm, x_hbm, w_hbm, v_hbm, b_hbm,
    sums_hbm, degree_hbm, self_hbm, place_hbm, pick_hbm,
    rows_v, count_v, adj, table, live, x, w, v, b, sums, degree, own_term, place, pick, sems,
):
    nodes = x.shape[0]
    small = [start(rows_hbm, rows_v, sems.at[0]), start(count_hbm, count_v, sems.at[1])]
    loads = [
        start(adj_hbm.at[pl.ds(0, nodes)], adj, sems.at[2]),
        start(table_hbm, table, sems.at[3]),
        start(live_hbm, live, sems.at[4]),
        start(x_hbm, x, sems.at[5]),
        start(w_hbm, w, sems.at[6]),
        start(b_hbm, b, sems.at[7]),
        start(v_hbm, v, sems.at[13]),
    ]
    finish(small)
    slot = slot_rows(rows_v, count_v, 2 * nodes)
    fill_pick(slot, pick)
    done = [start(pick, pick_hbm.at[:, pl.ds(0, nodes)], sems.at[8])]
    same = iota((128, 128), 0) == iota((128, 128), 1)
    for j in range(place.shape[1] // 128):
        lanes = slice(j * 128, (j + 1) * 128)
        wanted = jnp.sum(jnp.where(same, slot[lanes], 0.0), axis=0, keepdims=True)
        node = iota((nodes, 128), 0).astype(F32)
        place[:, lanes] = jnp.where(node == wanted, 1.0, 0.0).astype(BF)
    done.append(start(place, place_hbm, sems.at[9]))
    finish(loads)
    done.append(start(v, pick_hbm.at[:, pl.ds(nodes, v.shape[1])], sems.at[14]))
    ones = jnp.ones((nodes, 128), BF)
    for k, rows in enumerate(chunks(nodes)):
        total = (
            dot(adj[rows, :nodes], x[...]) + dot(adj[rows, nodes:], table[...]) + x[rows, :].astype(F32)
        )
        sums[rows, :] = dot(total.astype(BF), v[...])
        degree[rows, :] = dot(adj[rows, :nodes], ones) + dot(adj[rows, nodes:], live[...]) + 1.0
        own_term[rows, :] = dot(x[rows, :], w[...]) + b[...]
    done += [
        start(sums, sums_hbm, sems.at[10]),
        start(degree, degree_hbm, sems.at[11]),
        start(own_term, self_hbm, sems.at[12]),
    ]
    finish(done)


def own_second(
    adj_hbm, table_hbm, x_hbm, inverse_hbm, w_hbm, v_hbm, b_hbm, self_hbm,
    adj, table, x, inverse, w, v, b, own_term, sems,
):
    nodes = x.shape[0]
    pairs = zip(
        (adj_hbm.at[pl.ds(0, nodes)], table_hbm, x_hbm, inverse_hbm, w_hbm, v_hbm, b_hbm),
        (adj, table, x, inverse, w, v, b),
    )
    finish([start(src, dst, sems.at[k]) for k, (src, dst) in enumerate(pairs)])
    done = []
    for k, rows in enumerate(chunks(nodes)):
        total = (
            dot(adj[rows, :nodes], x[...]) + dot(adj[rows, nodes:], table[...]) + x[rows, :].astype(F32)
        )
        mean = scaled(total, inverse[rows, :]).astype(BF)
        own_term[rows, :] = dot(x[rows, :], w[...]) + dot(mean, v[...]) + b[...]
        done.append(start(own_term.at[rows], self_hbm.at[rows], sems.at[7 + k]))
    finish(done)


def mirror_part(adj_hbm, x_hbm, part_hbm, adj, x, part, sems):
    size, own = adj.shape
    loads = [
        start(adj_hbm.at[pl.ds(own, size), pl.ds(0, own)], adj, sems.at[0]),
        start(x_hbm, x, sems.at[1]),
    ]
    finish(loads)
    for k, rows in enumerate(chunks(size)):
        part[rows, :] = dot(adj[rows, :], x[...])
    start(part, part_hbm, sems.at[2]).wait()


def scaled(sums, inverse):
    return jnp.concatenate([tile * inverse for tile in lane_tiles(sums)], axis=1)


def first_end(
    packed, place_hbm, degree_hbm, sums_hbm, self_hbm, pick_hbm,
    hidden_hbm, inverse_hbm, out_hbm,
    place, degree, sums, w, own_term, pick, hidden, inverse, back, mixed, out, sems, sum_sems, self_sems,
):
    nodes = pick.shape[1]
    weights = start(pick_hbm.at[:, pl.ds(nodes, w.shape[1])], w, sems.at[0])
    need = [start(place_hbm, place, sems.at[1]), start(degree_hbm, degree, sems.at[2])]
    steps = chunks(hidden.shape[0])
    own = [
        [
            start(sums_hbm.at[rows], sums.at[rows], sum_sems.at[k]),
            start(self_hbm.at[rows], own_term.at[rows], self_sems.at[k]),
        ]
        for k, rows in enumerate(steps)
    ]
    picks = start(pick_hbm.at[:, pl.ds(0, nodes)], pick, sems.at[3])
    width = hidden.shape[1]
    for c in range(width // 128):
        back[:, c * 128 : (c + 1) * 128] = unpack_fours(packed, c).astype(BF)
    mixed[:, width:] = unpack_fours(packed, width // 128).astype(BF)
    weights.wait()
    mixed[:, :width] = dot(back[...], w[...]).astype(BF)
    finish(need)
    for k, rows in enumerate(steps):
        returned = dot(place[rows, :], mixed[...])
        edges = returned[:, width:]
        other = pltpu.roll(edges, 64, 1)
        low = iota(edges.shape, 1) < 64
        edges = jnp.where(low, 128.0 * edges + other, edges + 128.0 * other)
        finish(own[k])
        scale = 1.0 / (degree[rows, :] + edges)
        inverse[rows, :] = scale
        pre = own_term[rows, :] + scaled(sums[rows, :] + returned[:, :width], scale)
        hidden[rows, :] = jnp.maximum(pre, 0.0).astype(BF)
    done = [start(hidden, hidden_hbm, sems.at[4]), start(inverse, inverse_hbm, sems.at[5])]
    picks.wait()
    for k, rows in enumerate(chunks(pick.shape[0])):
        pair = rows.start // 8
        pack(lane_tiles(dot(pick[rows, :], hidden[...])), out, pair)
        here = pl.ds(pair, STEP // 8)
        done.append(start(out.at[here], out_hbm.at[here], sems.at[6 + k]))
    finish(done)


def second_end(
    packed, place_hbm, inverse_hbm, w_hbm, self_hbm, out_hbm,
    place, inverse, w, own_term, back, mixed, out, sems, self_sems,
):
    weights = start(w_hbm, w, sems.at[0])
    need = [start(place_hbm, place, sems.at[1]), start(inverse_hbm, inverse, sems.at[2])]
    steps = chunks(out.shape[0])
    own = [start(self_hbm.at[rows], own_term.at[rows], self_sems.at[k]) for k, rows in enumerate(steps)]
    unpack_into(packed, back)
    weights.wait()
    mixed[...] = dot(back[...], w[...]).astype(BF)
    finish(need)
    done = []
    for k, rows in enumerate(steps):
        returned = scaled(dot(place[rows, :], mixed[...]), inverse[rows, :])
        own[k].wait()
        out[rows, :] = (own_term[rows, :] + returned).astype(BF)
        done.append(start(out.at[rows], out_hbm.at[rows], sems.at[3 + k]))
    finish(done)


def array(*shape, dtype=F32):
    return jax.ShapeDtypeStruct(shape, dtype)


def call(kernel, outs, buffers, sems, flops, *in_specs):
    def run(*operands):
        held = [x for x, spec in zip(operands, in_specs) if spec is VMEM]
        room = sum(x.size * x.dtype.itemsize for x in held)
        spare = 200_000 if kernel is first_end else 0
        limit = ALL if kernel is first_gather else LIMIT - room - spare
        return pl.pallas_call(
            kernel,
            name=kernel.__name__,
            in_specs=list(in_specs) + [HBM] * (len(operands) - len(in_specs)),
            out_specs=[HBM] * len(outs),
            out_shape=list(outs),
            scratch_shapes=[pltpu.VMEM(b.shape, b.dtype) for b in buffers]
            + [pltpu.SemaphoreType.DMA((n,)) for n in sems],
            cost_estimate=pl.CostEstimate(flops=flops, bytes_accessed=4 << 20, transcendentals=0),
            compiler_params=pltpu.CompilerParams(vmem_limit_bytes=limit),
        )(*operands)

    return run


def exchange(packed):
    sent = packed.reshape((-1,) + packed.shape[2:])
    if packed.shape[3] == 8:
        sent = packed.reshape(sent.shape[0], -1, 128)
    arrived = lax.all_to_all(sent, "vert", split_axis=0, concat_axis=0, tiled=True)
    return arrived.reshape(packed.shape)


def body(
    features, send_rows, mirror_count, tile_coord, tile_mask, tile_count,
    w_self1, w_neigh1, bias1, w_self2, w_neigh2, bias2,
):
    own, width = features.shape
    _, peers, slots = send_rows.shape
    block = tile_mask.shape[2]
    tiles = tile_mask.shape[1]
    mirrors = peers * slots
    rows = own + mirrors
    pairs = peers // 2
    message = array(pairs, 2, 2, 8, 128, dtype=BF)
    longer = array(pairs, 2, 5, 4, 128, dtype=BF)
    nodes = array(own, width, dtype=BF)
    wide = array(own, width)
    narrow = array(own, 128)
    weight = array(width, width, dtype=BF)
    bias = array(1, width)
    table_a = array(mirrors, width, dtype=BF)
    live_a = array(mirrors, 128, dtype=BF)
    part_a = array(mirrors, width)
    edges_a = array(mirrors, 128)
    adj_a = array(rows, rows, dtype=BF)
    adj_own = array(own, rows, dtype=BF)
    adj_mirror = array(mirrors, mirrors, dtype=BF)
    adj_to_mirror = array(mirrors, own, dtype=BF)
    pick_a = array(mirrors, own, dtype=BF)
    place_a = array(own, mirrors, dtype=BF)
    slot_a = array(slots, peers, dtype=jnp.int32)
    count_a = array(1, peers, dtype=jnp.int32)

    slot_table = send_rows[0].T
    bias1 = bias1.astype(F32).reshape(1, width)
    bias2 = bias2.astype(F32).reshape(1, width)

    (sent,) = call(
        first_gather, [message], [slot_a, count_a, nodes, pick_a, message], [5],
        2 * mirrors * own * width,
    )(slot_table, mirror_count, features)
    arrived = exchange(sent)

    adj, part, edges = call(
        build_adjacency, [adj_a, part_a, edges_a],
        [array(tiles, block, block, dtype=jnp.int32), nodes, adj_a, part_a, edges_a],
        [tiles // GROUP, 4], 4 * rows * own * width, SMEM, SMEM,
    )(tile_coord[0], tile_count, tile_mask[0], features)

    table, live, sent = call(
        mirror_first, [table_a, live_a, longer],
        [adj_mirror, part_a, edges_a, table_a, live_a, longer], [8],
        2 * mirrors * mirrors * width, VMEM,
    )(arrived, adj, part, edges)
    arrived = exchange(sent)

    sums, degree, own_term, place, pick = call(
        own_first, [wide, narrow, wide, place_a, array(mirrors, own + width, dtype=BF)],
        [
            slot_a, count_a, adj_own, table_a, live_a, nodes, weight, weight, bias,
            wide, narrow, wide, place_a, pick_a,
        ],
        [15], 4 * own * rows * width,
    )(slot_table, mirror_count, adj, table, live, features, w_self1, w_neigh1, bias1)

    hidden, inverse, sent = call(
        first_end, [nodes, narrow, message],
        [
            place_a, narrow, wide, weight, wide, pick_a,
            nodes, narrow, table_a, array(mirrors, width + 128, dtype=BF), message,
        ],
        [8, own // STEP, own // STEP], 6 * own * mirrors * width, VMEM,
    )(arrived, place, degree, sums, own_term, pick)
    arrived = exchange(sent)

    (part,) = call(
        mirror_part, [part_a], [adj_to_mirror, nodes, part_a], [3], 2 * mirrors * own * width
    )(adj, hidden)

    table, sent = call(
        mirror_second, [table_a, message], [adj_mirror, part_a, table_a, message], [6],
        2 * mirrors * mirrors * width, VMEM,
    )(arrived, adj, part)
    arrived = exchange(sent)

    (own_term,) = call(
        own_second, [wide],
        [adj_own, table_a, nodes, narrow, weight, weight, bias, wide], [7 + own // STEP],
        4 * own * rows * width,
    )(adj, table, hidden, inverse, w_self2, w_neigh2, bias2)

    (embedding,) = call(
        second_end, [nodes],
        [place_a, narrow, weight, wide, table_a, table_a, nodes], [3 + own // STEP, own // STEP],
        4 * own * mirrors * width, VMEM,
    )(arrived, place, inverse, w_neigh2, own_term)
    return embedding


def solution(mesh):
    in_specs = (
        P("vert", None),
        P("vert", None, None),
        P("vert", None),
        P("vert", None, None),
        P("vert", None, None, None),
        P("vert"),
        P(),
        P(),
        P(),
        P(),
        P(),
        P(),
    )
    out_specs = P("vert", None)
    return jax.shard_map(body, mesh=mesh, in_specs=in_specs, out_specs=out_specs, check_vma=False)
```

```python
import jax
import jax.numpy as jnp
from jax import lax
from jax.experimental import pallas as pl
from jax.experimental.pallas import tpu as pltpu
from jax.sharding import PartitionSpec as P

GROUP = 8
STEP = 256
DEAD = 64.0
LIMIT = 55_000_000
ALL = 63_400_000
BF = jnp.bfloat16
F32 = jnp.float32
HBM = pl.BlockSpec(memory_space=pltpu.HBM)
VMEM = pl.BlockSpec(memory_space=pltpu.VMEM)
SMEM = pl.BlockSpec(memory_space=pltpu.SMEM)


def dot(a, b):
    return jnp.dot(a, b, preferred_element_type=F32)


def iota(shape, axis):
    return lax.broadcasted_iota(jnp.int32, shape, axis)


def start(src, dst, sem):
    copy = pltpu.make_async_copy(src, dst, sem)
    copy.start()
    return copy


def finish(copies):
    for copy in copies:
        copy.wait()


def chunks(rows):
    return [slice(k, k + STEP) for k in range(0, rows, STEP)]


def pack(columns, out_ref, pair):
    pairs = columns[0].shape[0] // 8
    low = iota((pairs, 8, 128), 1) < 4
    for h in range(len(columns) // 2):
        first = columns[2 * h].reshape(pairs, 8, 128)
        second = columns[2 * h + 1].reshape(pairs, 8, 128)
        even = jnp.where(low, first, pltpu.roll(second, 4, 1))
        odd = jnp.where(low, pltpu.roll(first, 4, 1), second)
        out_ref[pair : pair + pairs, 0, h] = even.astype(BF)
        out_ref[pair : pair + pairs, 1, h] = odd.astype(BF)


def unpack(in_ref, h):
    pairs = in_ref.shape[0]
    low = iota((pairs, 8, 128), 1) < 4
    even = in_ref[:, 0, h].astype(F32)
    odd = in_ref[:, 1, h].astype(F32)
    first = jnp.where(low, even, pltpu.roll(odd, 4, 1))
    second = jnp.where(low, pltpu.roll(even, 4, 1), odd)
    return first.reshape(pairs * 8, 128), second.reshape(pairs * 8, 128)


def unpack_into(in_ref, table_ref):
    for h in range(in_ref.shape[2]):
        for c, tile in zip((2 * h, 2 * h + 1), unpack(in_ref, h)):
            table_ref[:, c * 128 : (c + 1) * 128] = tile.astype(BF)


def pack_fours(columns, out_ref, pair):
    pairs = columns[0].shape[0] // 8
    for c, column in enumerate(columns):
        both = column.reshape(pairs, 8, 128).astype(BF)
        out_ref[pair : pair + pairs, 0, c] = both[:, :4]
        out_ref[pair : pair + pairs, 1, c] = both[:, 4:]


def unpack_fours(in_ref, c):
    both = jnp.concatenate([in_ref[:, 0, c].astype(F32), in_ref[:, 1, c].astype(F32)], axis=1)
    return both.reshape(-1, 128)


def lane_tiles(array):
    return [array[:, c * 128 : (c + 1) * 128] for c in range(array.shape[1] // 128)]


def slot_rows(rows_ref, count_ref, never):
    slots, peers = rows_ref.shape
    live = iota((slots, peers), 0) < count_ref[...]
    value = jnp.where(live, rows_ref[...], never).astype(F32)
    value = jnp.concatenate([value, value], axis=0)
    shape = (peers // 2, 2 * slots, peers)
    row = iota(shape, 0) * 2 * slots + iota(shape, 1)
    mine = row // slots == iota(shape, 2)
    picked = jnp.where(mine, value[None], 0.0).reshape(peers * slots, peers)
    return jnp.sum(picked, axis=1, keepdims=True)


def fill_pick(slot, pick_ref):
    for j in range(pick_ref.shape[1] // 128):
        node = (iota((pick_ref.shape[0], 128), 1) + j * 128).astype(F32)
        pick_ref[:, j * 128 : (j + 1) * 128] = jnp.where(slot == node, 1.0, 0.0).astype(BF)


def first_gather(rows_hbm, count_hbm, x_hbm, out_hbm, rows, count, x, pick, out, sems):
    small = [start(rows_hbm, rows, sems.at[0]), start(count_hbm, count, sems.at[1])]
    features = start(x_hbm, x, sems.at[2])
    finish(small)
    nodes = x.shape[0]
    slot = slot_rows(rows, count, 2 * nodes)
    fill_pick(slot, pick)
    features.wait()
    done = []
    for k, part in enumerate(chunks(pick.shape[0])):
        picked = dot(pick[part, :], x[...])
        dead = slot[part] >= nodes
        pair = part.start // 8
        pack([jnp.where(dead, DEAD, tile) for tile in lane_tiles(picked)], out, pair)
        here = pl.ds(pair, STEP // 8)
        done.append(start(out.at[here], out_hbm.at[here], sems.at[3 + k]))
    finish(done)


def build_adjacency(
    coord, count, mask_hbm, x_hbm, adj_hbm, part_hbm, edges_hbm,
    mask, x, adj, part, edges, mask_sems, sems,
):
    live = count[0]
    groups = (live + GROUP - 1) // GROUP

    def group_copy(g):
        here = pl.ds(g * GROUP, GROUP)
        return pltpu.make_async_copy(mask_hbm.at[here], mask.at[here], mask_sems.at[g])

    lax.fori_loop(0, groups, lambda g, c: (group_copy(g).start(), c)[1], 0)
    features = start(x_hbm, x, sems.at[0])
    adj[...] = jnp.zeros_like(adj)

    def add_group(g, carry):
        group_copy(g).wait()
        for j in range(GROUP):
            tile = g * GROUP + j

            @pl.when(tile < live)
            def _(tile=tile):
                to = pl.ds(pl.multiple_of(coord[0, tile] * 128, 128), 128)
                src = pl.ds(pl.multiple_of(coord[1, tile] * 128, 128), 128)
                adj[to, src] += mask[tile].astype(F32).astype(BF)

        return carry

    lax.fori_loop(0, groups, add_group, 0)
    done = [start(adj, adj_hbm, sems.at[1])]
    features.wait()
    own = x.shape[0]
    ones = jnp.ones((own, 128), BF)
    for k, rows in enumerate(chunks(part.shape[0])):
        source = adj[own + rows.start : own + rows.stop, :own]
        part[rows, :] = dot(source, x[...])
        edges[rows, :] = dot(source, ones)
    done += [start(part, part_hbm, sems.at[2]), start(edges, edges_hbm, sems.at[3])]
    finish(done)


def mirror_first(
    packed, adj_hbm, part_hbm, edges_hbm, table_hbm, live_hbm, out_hbm,
    adj, part, edges, table, live, out, sems,
):
    size = adj.shape[0]
    own = adj_hbm.shape[0] - size
    weights = start(adj_hbm.at[pl.ds(own, size), pl.ds(own, size)], adj, sems.at[1])
    rest = [start(part_hbm, part, sems.at[2]), start(edges_hbm, edges, sems.at[3])]
    for h in range(packed.shape[2]):
        for c, tile in zip((2 * h, 2 * h + 1), unpack(packed, h)):
            dead = tile > DEAD / 2
            table[:, c * 128 : (c + 1) * 128] = jnp.where(dead, 0.0, tile).astype(BF)
            if c == 0:
                live[...] = jnp.where(dead, 0.0, 1.0).astype(BF)
    done = [start(table, table_hbm, sems.at[4]), start(live, live_hbm, sems.at[5])]
    weights.wait()
    finish(rest)
    for k, rows in enumerate(chunks(size)):
        sums = part[rows, :] + dot(adj[rows, :], table[...])
        total = edges[rows, :] + dot(adj[rows, :], live[...])
        high = jnp.floor(total * (1.0 / 128.0))
        pair = rows.start // 8
        low = iota(total.shape, 1) < 64
        pack_fours(lane_tiles(sums) + [jnp.where(low, high, total - 128.0 * high)], out, pair)
        here = pl.ds(pair, STEP // 8)
        done.append(start(out.at[here], out_hbm.at[here], sems.at[6 + k]))
    finish(done)


def mirror_second(packed, adj_hbm, part_hbm, table_hbm, out_hbm, adj, part, table, out, sems):
    size = adj.shape[0]
    own = adj_hbm.shape[0] - size
    rest = [
        start(adj_hbm.at[pl.ds(own, size), pl.ds(own, size)], adj, sems.at[1]),
        start(part_hbm, part, sems.at[2]),
    ]
    unpack_into(packed, table)
    done = [start(table, table_hbm, sems.at[3])]
    finish(rest)
    for k, rows in enumerate(chunks(size)):
        sums = part[rows, :] + dot(adj[rows, :], table[...])
        pair = rows.start // 8
        pack(lane_tiles(sums), out, pair)
        here = pl.ds(pair, STEP // 8)
        done.append(start(out.at[here], out_hbm.at[here], sems.at[4 + k]))
    finish(done)


def own_first(
    rows_hbm, count_hbm, adj_hbm, table_hbm, live_hbm, x_hbm, w_hbm, v_hbm, b_hbm,
    rounded_hbm, degree_hbm, place_hbm, near_hbm, near_sums_hbm, near_degree_hbm, near_self_hbm,
    rows_v, count_v, adj, table, live, x, w, v, b, degree, place, near, near_sums, near_degree,
    near_self, pick, rounded, sems,
):
    nodes = x.shape[0]
    small = [start(rows_hbm, rows_v, sems.at[0]), start(count_hbm, count_v, sems.at[1])]
    loads = [
        start(adj_hbm.at[pl.ds(0, nodes)], adj, sems.at[2]),
        start(table_hbm, table, sems.at[3]),
        start(live_hbm, live, sems.at[4]),
        start(x_hbm, x, sems.at[5]),
        start(w_hbm, w, sems.at[6]),
        start(b_hbm, b, sems.at[7]),
        start(v_hbm, v, sems.at[13]),
    ]
    finish(small)
    slot = slot_rows(rows_v, count_v, 2 * nodes)
    fill_pick(slot, pick)
    done = []
    same = iota((128, 128), 0) == iota((128, 128), 1)
    for j in range(place.shape[1] // 128):
        lanes = slice(j * 128, (j + 1) * 128)
        wanted = jnp.sum(jnp.where(same, slot[lanes], 0.0), axis=0, keepdims=True)
        node = iota((nodes, 128), 0).astype(F32)
        place[:, lanes] = jnp.where(node == wanted, 1.0, 0.0).astype(BF)
    done.append(start(place, place_hbm, sems.at[9]))
    finish(loads)
    size = near.shape[0]
    done.append(start(v, near_hbm.at[:, pl.ds(size, v.shape[1])], sems.at[14]))
    ones = jnp.ones((nodes, 128), BF)
    for k, rows in enumerate(chunks(nodes)):
        total = (
            dot(adj[rows, :nodes], x[...]) + dot(adj[rows, nodes:], table[...]) + x[rows, :].astype(F32)
        )
        rounded[rows, :] = total.astype(BF)
        degree[rows, :] = dot(adj[rows, :nodes], ones) + dot(adj[rows, nodes:], live[...]) + 1.0
    done += [
        start(rounded, rounded_hbm, sems.at[10]),
        start(degree, degree_hbm, sems.at[11]),
    ]
    high = jnp.floor(degree[...] * (1.0 / 128.0))
    low = (degree[...] - 128.0 * high).astype(BF)
    high = high.astype(BF)
    for k, rows in enumerate(chunks(size)):
        dead = slot[rows] >= nodes
        mine = pick[rows, :]
        own_rows = dot(mine, x[...]).astype(BF)
        near_self[rows, :] = jnp.where(dead, -1e30, dot(own_rows, w[...]) + b[...])
        near_sums[rows, :] = dot(dot(mine, rounded[...]).astype(BF), v[...])
        near_degree[rows, :] = jnp.where(dead, 1.0, 128.0 * dot(mine, high) + dot(mine, low))
        near[rows, :] = dot(mine, place[...]).astype(BF)
    done += [
        start(near, near_hbm.at[:, pl.ds(0, size)], sems.at[8]),
        start(near_sums, near_sums_hbm, sems.at[15]),
        start(near_degree, near_degree_hbm, sems.at[16]),
        start(near_self, near_self_hbm, sems.at[17]),
    ]
    finish(done)


def own_second(
    adj_hbm, table_hbm, x_hbm, inverse_hbm, w_hbm, v_hbm, b_hbm, self_hbm,
    adj, table, x, inverse, w, v, b, own_term, sems,
):
    nodes = x.shape[0]
    pairs = zip(
        (adj_hbm.at[pl.ds(0, nodes)], table_hbm, x_hbm, inverse_hbm, w_hbm, v_hbm, b_hbm),
        (adj, table, x, inverse, w, v, b),
    )
    finish([start(src, dst, sems.at[k]) for k, (src, dst) in enumerate(pairs)])
    done = []
    for k, rows in enumerate(chunks(nodes)):
        total = (
            dot(adj[rows, :nodes], x[...]) + dot(adj[rows, nodes:], table[...]) + x[rows, :].astype(F32)
        )
        mean = scaled(total, inverse[rows, :]).astype(BF)
        own_term[rows, :] = dot(x[rows, :], w[...]) + dot(mean, v[...]) + b[...]
        done.append(start(own_term.at[rows], self_hbm.at[rows], sems.at[7 + k]))
    finish(done)


def scaled(sums, inverse):
    return jnp.concatenate([tile * inverse for tile in lane_tiles(sums)], axis=1)


def layer_rows(select, mixed, degree, sums, own_term):
    width = own_term.shape[1]
    returned = dot(select, mixed)
    edges = returned[:, width:]
    other = pltpu.roll(edges, 64, 1)
    low = iota(edges.shape, 1) < 64
    scale = 1.0 / (degree + jnp.where(low, 128.0 * edges + other, edges + 128.0 * other))
    return jnp.maximum(own_term + scaled(sums + returned[:, :width], scale), 0.0), scale


def first_end(
    packed, degree_hbm, sums_hbm, self_hbm, near_hbm, mixed_hbm, out_hbm,
    degree, sums, w, own_term, near, back, mixed, out, sems,
):
    size, width = own_term.shape
    weights = start(near_hbm.at[:, pl.ds(size, width)], w, sems.at[0])
    need = [
        start(near_hbm.at[:, pl.ds(0, size)], near, sems.at[1]),
        start(degree_hbm, degree, sems.at[2]),
        start(sums_hbm, sums, sems.at[3]),
        start(self_hbm, own_term, sems.at[4]),
    ]
    for c in range(width // 128):
        back[:, c * 128 : (c + 1) * 128] = unpack_fours(packed, c).astype(BF)
    mixed[:, width:] = unpack_fours(packed, width // 128).astype(BF)
    weights.wait()
    mixed[:, :width] = dot(back[...], w[...]).astype(BF)
    done = [start(mixed, mixed_hbm.at[:, pl.ds(0, mixed.shape[1])], sems.at[5])]
    finish(need)
    for k, rows in enumerate(chunks(size)):
        hidden, _ = layer_rows(near[rows, :], mixed[...], degree[rows, :], sums[rows, :], own_term[rows, :])
        pair = rows.start // 8
        pack(lane_tiles(hidden), out, pair)
        here = pl.ds(pair, STEP // 8)
        done.append(start(out.at[here], out_hbm.at[here], sems.at[6 + k]))
    finish(done)


def hidden_rows(
    place_hbm, mixed_hbm, degree_hbm, rounded_hbm, x_hbm, w_hbm, v_hbm, b_hbm, adj_hbm,
    hidden_hbm, inverse_hbm, part_hbm,
    place, mixed, degree, rounded, x, w, v, b, adj, hidden, inverse, part, sems,
):
    size, own = adj.shape
    pairs = zip(
        (
            place_hbm, mixed_hbm.at[:, pl.ds(0, mixed.shape[1])], degree_hbm, rounded_hbm,
            x_hbm, w_hbm, v_hbm, b_hbm, adj_hbm.at[pl.ds(own, size), pl.ds(0, own)],
        ),
        (place, mixed, degree, rounded, x, w, v, b, adj),
    )
    finish([start(src, dst, sems.at[k]) for k, (src, dst) in enumerate(pairs)])
    for k, rows in enumerate(chunks(own)):
        value, inverse[rows, :] = layer_rows(
            place[rows, :], mixed[...], degree[rows, :],
            dot(rounded[rows, :], v[...]), dot(x[rows, :], w[...]) + b[...],
        )
        hidden[rows, :] = value.astype(BF)
    done = [start(hidden, hidden_hbm, sems.at[9]), start(inverse, inverse_hbm, sems.at[10])]
    for k, rows in enumerate(chunks(size)):
        part[rows, :] = dot(adj[rows, :], hidden[...])
    done.append(start(part, part_hbm, sems.at[11]))
    finish(done)


def second_end(
    packed, place_hbm, inverse_hbm, w_hbm, self_hbm, out_hbm,
    place, inverse, w, own_term, back, mixed, out, sems, self_sems,
):
    weights = start(w_hbm, w, sems.at[0])
    need = [start(place_hbm, place, sems.at[1]), start(inverse_hbm, inverse, sems.at[2])]
    steps = chunks(out.shape[0])
    own = [start(self_hbm.at[rows], own_term.at[rows], self_sems.at[k]) for k, rows in enumerate(steps)]
    unpack_into(packed, back)
    weights.wait()
    mixed[...] = dot(back[...], w[...]).astype(BF)
    finish(need)
    done = []
    for k, rows in enumerate(steps):
        returned = scaled(dot(place[rows, :], mixed[...]), inverse[rows, :])
        own[k].wait()
        out[rows, :] = (own_term[rows, :] + returned).astype(BF)
        done.append(start(out.at[rows], out_hbm.at[rows], sems.at[3 + k]))
    finish(done)


def array(*shape, dtype=F32):
    return jax.ShapeDtypeStruct(shape, dtype)


def call(kernel, outs, buffers, sems, flops, *in_specs):
    def run(*operands):
        held = [x for x, spec in zip(operands, in_specs) if spec is VMEM]
        room = sum(x.size * x.dtype.itemsize for x in held)
        spare = 200_000 if kernel is first_end else 0
        limit = ALL if kernel is first_gather else LIMIT - room - spare
        return pl.pallas_call(
            kernel,
            name=kernel.__name__,
            in_specs=list(in_specs) + [HBM] * (len(operands) - len(in_specs)),
            out_specs=[HBM] * len(outs),
            out_shape=list(outs),
            scratch_shapes=[pltpu.VMEM(b.shape, b.dtype) for b in buffers]
            + [pltpu.SemaphoreType.DMA((n,)) for n in sems],
            cost_estimate=pl.CostEstimate(flops=flops, bytes_accessed=4 << 20, transcendentals=0),
            compiler_params=pltpu.CompilerParams(vmem_limit_bytes=limit),
        )(*operands)

    return run


def exchange(packed):
    sent = packed.reshape((-1,) + packed.shape[2:])
    if packed.shape[3] == 8:
        sent = packed.reshape(sent.shape[0], -1, 128)
    arrived = lax.all_to_all(sent, "vert", split_axis=0, concat_axis=0, tiled=True)
    return arrived.reshape(packed.shape)


def body(
    features, send_rows, mirror_count, tile_coord, tile_mask, tile_count,
    w_self1, w_neigh1, bias1, w_self2, w_neigh2, bias2,
):
    own, width = features.shape
    _, peers, slots = send_rows.shape
    block = tile_mask.shape[2]
    tiles = tile_mask.shape[1]
    mirrors = peers * slots
    rows = own + mirrors
    pairs = peers // 2
    message = array(pairs, 2, 2, 8, 128, dtype=BF)
    longer = array(pairs, 2, 5, 4, 128, dtype=BF)
    nodes = array(own, width, dtype=BF)
    wide = array(own, width)
    narrow = array(own, 128)
    weight = array(width, width, dtype=BF)
    bias = array(1, width)
    table_a = array(mirrors, width, dtype=BF)
    live_a = array(mirrors, 128, dtype=BF)
    part_a = array(mirrors, width)
    edges_a = array(mirrors, 128)
    adj_a = array(rows, rows, dtype=BF)
    adj_own = array(own, rows, dtype=BF)
    adj_mirror = array(mirrors, mirrors, dtype=BF)
    adj_to_mirror = array(mirrors, own, dtype=BF)
    pick_a = array(mirrors, own, dtype=BF)
    place_a = array(own, mirrors, dtype=BF)
    slot_a = array(slots, peers, dtype=jnp.int32)
    count_a = array(1, peers, dtype=jnp.int32)

    slot_table = send_rows[0].T
    bias1 = bias1.astype(F32).reshape(1, width)
    bias2 = bias2.astype(F32).reshape(1, width)

    (sent,) = call(
        first_gather, [message], [slot_a, count_a, nodes, pick_a, message], [5],
        2 * mirrors * own * width,
    )(slot_table, mirror_count, features)
    arrived = exchange(sent)

    adj, part, edges = call(
        build_adjacency, [adj_a, part_a, edges_a],
        [array(tiles, block, block, dtype=jnp.int32), nodes, adj_a, part_a, edges_a],
        [tiles // GROUP, 4], 4 * rows * own * width, SMEM, SMEM,
    )(tile_coord[0], tile_count, tile_mask[0], features)

    table, live, sent = call(
        mirror_first, [table_a, live_a, longer],
        [adj_mirror, part_a, edges_a, table_a, live_a, longer], [8],
        2 * mirrors * mirrors * width, VMEM,
    )(arrived, adj, part, edges)
    arrived = exchange(sent)

    near_w = array(mirrors, mirrors + width, dtype=BF)
    rounded, degree, place, near, near_sums, near_degree, near_self = call(
        own_first, [nodes, narrow, place_a, near_w, part_a, edges_a, part_a],
        [
            slot_a, count_a, adj_own, table_a, live_a, nodes, weight, weight, bias,
            narrow, place_a, adj_mirror, part_a, edges_a, part_a, pick_a, nodes,
        ],
        [18], 6 * own * rows * width,
    )(slot_table, mirror_count, adj, table, live, features, w_self1, w_neigh1, bias1)

    mixed_a = array(mirrors, width + 128, dtype=BF)
    mixed, sent = call(
        first_end, [array(mirrors, 2 * width, dtype=BF), message],
        [edges_a, part_a, weight, part_a, adj_mirror, table_a, mixed_a, message], [8],
        4 * mirrors * mirrors * width, VMEM,
    )(arrived, near_degree, near_sums, near_self, near)
    arrived = exchange(sent)

    hidden, inverse, part = call(
        hidden_rows, [nodes, narrow, part_a],
        [
            place_a, mixed_a, narrow, nodes, nodes, weight, weight, bias, adj_to_mirror,
            nodes, narrow, part_a,
        ],
        [12], 4 * own * mirrors * width,
    )(place, mixed, degree, rounded, features, w_self1, w_neigh1, bias1, adj)

    table, sent = call(
        mirror_second, [table_a, message], [adj_mirror, part_a, table_a, message], [6],
        2 * mirrors * mirrors * width, VMEM,
    )(arrived, adj, part)
    arrived = exchange(sent)

    (own_term,) = call(
        own_second, [wide],
        [adj_own, table_a, nodes, narrow, weight, weight, bias, wide], [7 + own // STEP],
        4 * own * rows * width,
    )(adj, table, hidden, inverse, w_self2, w_neigh2, bias2)

    (embedding,) = call(
        second_end, [nodes],
        [place_a, narrow, weight, wide, table_a, table_a, nodes], [3 + own // STEP, own // STEP],
        4 * own * mirrors * width, VMEM,
    )(arrived, place, inverse, w_neigh2, own_term)
    return embedding


def solution(mesh):
    in_specs = (
        P("vert", None),
        P("vert", None, None),
        P("vert", None),
        P("vert", None, None),
        P("vert", None, None, None),
        P("vert"),
        P(),
        P(),
        P(),
        P(),
        P(),
        P(),
    )
    out_specs = P("vert", None)
    return jax.shard_map(body, mesh=mesh, in_specs=in_specs, out_specs=out_specs, check_vma=False)
```

```python
import jax
import jax.numpy as jnp
from jax import lax
from jax.experimental import pallas as pl
from jax.experimental.pallas import tpu as pltpu
from jax.sharding import PartitionSpec as P

GROUP = 8
STEP = 256
DEAD = 64.0
LIMIT = 55_000_000
ALL = 63_400_000
BF = jnp.bfloat16
F32 = jnp.float32
HBM = pl.BlockSpec(memory_space=pltpu.HBM)
VMEM = pl.BlockSpec(memory_space=pltpu.VMEM)
SMEM = pl.BlockSpec(memory_space=pltpu.SMEM)


def dot(a, b):
    return jnp.dot(a, b, preferred_element_type=F32)


def iota(shape, axis):
    return lax.broadcasted_iota(jnp.int32, shape, axis)


def start(src, dst, sem):
    copy = pltpu.make_async_copy(src, dst, sem)
    copy.start()
    return copy


def finish(copies):
    for copy in copies:
        copy.wait()


def chunks(rows):
    return [slice(k, k + STEP) for k in range(0, rows, STEP)]


def pack(columns, out_ref, pair):
    pairs = columns[0].shape[0] // 8
    low = iota((pairs, 8, 128), 1) < 4
    for h in range(len(columns) // 2):
        first = columns[2 * h].reshape(pairs, 8, 128)
        second = columns[2 * h + 1].reshape(pairs, 8, 128)
        even = jnp.where(low, first, pltpu.roll(second, 4, 1))
        odd = jnp.where(low, pltpu.roll(first, 4, 1), second)
        out_ref[pair : pair + pairs, 0, h] = even.astype(BF)
        out_ref[pair : pair + pairs, 1, h] = odd.astype(BF)


def unpack(in_ref, h):
    pairs = in_ref.shape[0]
    low = iota((pairs, 8, 128), 1) < 4
    even = in_ref[:, 0, h].astype(F32)
    odd = in_ref[:, 1, h].astype(F32)
    first = jnp.where(low, even, pltpu.roll(odd, 4, 1))
    second = jnp.where(low, pltpu.roll(even, 4, 1), odd)
    return first.reshape(pairs * 8, 128), second.reshape(pairs * 8, 128)


def unpack_into(in_ref, table_ref):
    for h in range(in_ref.shape[2]):
        for c, tile in zip((2 * h, 2 * h + 1), unpack(in_ref, h)):
            table_ref[:, c * 128 : (c + 1) * 128] = tile.astype(BF)


def pack_fours(columns, out_ref, pair):
    pairs = columns[0].shape[0] // 8
    for c, column in enumerate(columns):
        both = column.reshape(pairs, 8, 128).astype(BF)
        out_ref[pair : pair + pairs, 0, c] = both[:, :4]
        out_ref[pair : pair + pairs, 1, c] = both[:, 4:]


def unpack_fours(in_ref, c):
    both = jnp.concatenate([in_ref[:, 0, c].astype(F32), in_ref[:, 1, c].astype(F32)], axis=1)
    return both.reshape(-1, 128)


def lane_tiles(array):
    return [array[:, c * 128 : (c + 1) * 128] for c in range(array.shape[1] // 128)]


def slot_rows(rows_ref, count_ref, never):
    slots, peers = rows_ref.shape
    live = iota((slots, peers), 0) < count_ref[...]
    value = jnp.where(live, rows_ref[...], never).astype(F32)
    value = jnp.concatenate([value, value], axis=0)
    shape = (peers // 2, 2 * slots, peers)
    row = iota(shape, 0) * 2 * slots + iota(shape, 1)
    mine = row // slots == iota(shape, 2)
    picked = jnp.where(mine, value[None], 0.0).reshape(peers * slots, peers)
    return jnp.sum(picked, axis=1, keepdims=True)


def fill_pick(slot, pick_ref):
    for j in range(pick_ref.shape[1] // 128):
        node = (iota((pick_ref.shape[0], 128), 1) + j * 128).astype(F32)
        pick_ref[:, j * 128 : (j + 1) * 128] = jnp.where(slot == node, 1.0, 0.0).astype(BF)


def first_gather(rows_hbm, count_hbm, x_hbm, out_hbm, rows, count, x, pick, out, sems):
    small = [start(rows_hbm, rows, sems.at[0]), start(count_hbm, count, sems.at[1])]
    features = start(x_hbm, x, sems.at[2])
    finish(small)
    nodes = x.shape[0]
    slot = slot_rows(rows, count, 2 * nodes)
    fill_pick(slot, pick)
    features.wait()
    done = []
    for k, part in enumerate(chunks(pick.shape[0])):
        picked = dot(pick[part, :], x[...])
        dead = slot[part] >= nodes
        pair = part.start // 8
        pack([jnp.where(dead, DEAD, tile) for tile in lane_tiles(picked)], out, pair)
        here = pl.ds(pair, STEP // 8)
        done.append(start(out.at[here], out_hbm.at[here], sems.at[3 + k]))
    finish(done)


def build_adjacency(
    coord, count, mask_hbm, x_hbm, adj_hbm, part_hbm, edges_hbm,
    mask, x, adj, part, edges, mask_sems, sems,
):
    live = count[0]
    groups = (live + GROUP - 1) // GROUP

    def group_copy(g):
        here = pl.ds(g * GROUP, GROUP)
        return pltpu.make_async_copy(mask_hbm.at[here], mask.at[here], mask_sems.at[g])

    lax.fori_loop(0, groups, lambda g, c: (group_copy(g).start(), c)[1], 0)
    features = start(x_hbm, x, sems.at[0])
    adj[...] = jnp.zeros_like(adj)

    def add_group(g, carry):
        group_copy(g).wait()
        for j in range(GROUP):
            tile = g * GROUP + j

            @pl.when(tile < live)
            def _(tile=tile):
                to = pl.ds(pl.multiple_of(coord[0, tile] * 128, 128), 128)
                src = pl.ds(pl.multiple_of(coord[1, tile] * 128, 128), 128)
                adj[to, src] += mask[tile].astype(F32).astype(BF)

        return carry

    lax.fori_loop(0, groups, add_group, 0)
    done = [start(adj, adj_hbm, sems.at[1])]
    features.wait()
    own = x.shape[0]
    ones = jnp.ones((own, 128), BF)
    for k, rows in enumerate(chunks(part.shape[0])):
        source = adj[own + rows.start : own + rows.stop, :own]
        part[rows, :] = dot(source, x[...])
        edges[rows, :] = dot(source, ones)
    done += [start(part, part_hbm, sems.at[2]), start(edges, edges_hbm, sems.at[3])]
    finish(done)


def mirror_first(
    packed, adj_hbm, part_hbm, edges_hbm, table_hbm, live_hbm, out_hbm,
    adj, part, edges, table, live, out, sems,
):
    size = adj.shape[0]
    own = adj_hbm.shape[0] - size
    weights = start(adj_hbm.at[pl.ds(own, size), pl.ds(own, size)], adj, sems.at[1])
    rest = [start(part_hbm, part, sems.at[2]), start(edges_hbm, edges, sems.at[3])]
    for h in range(packed.shape[2]):
        for c, tile in zip((2 * h, 2 * h + 1), unpack(packed, h)):
            dead = tile > DEAD / 2
            table[:, c * 128 : (c + 1) * 128] = jnp.where(dead, 0.0, tile).astype(BF)
            if c == 0:
                live[...] = jnp.where(dead, 0.0, 1.0).astype(BF)
    done = [start(table, table_hbm, sems.at[4]), start(live, live_hbm, sems.at[5])]
    weights.wait()
    finish(rest)
    for k, rows in enumerate(chunks(size)):
        sums = part[rows, :] + dot(adj[rows, :], table[...])
        total = edges[rows, :] + dot(adj[rows, :], live[...])
        high = jnp.floor(total * (1.0 / 128.0))
        pair = rows.start // 8
        low = iota(total.shape, 1) < 64
        pack_fours(lane_tiles(sums) + [jnp.where(low, high, total - 128.0 * high)], out, pair)
        here = pl.ds(pair, STEP // 8)
        done.append(start(out.at[here], out_hbm.at[here], sems.at[6 + k]))
    finish(done)


def mirror_second(packed, adj_hbm, part_hbm, table_hbm, out_hbm, adj, part, table, out, sems):
    size = adj.shape[0]
    own = adj_hbm.shape[0] - size
    rest = [
        start(adj_hbm.at[pl.ds(own, size), pl.ds(own, size)], adj, sems.at[1]),
        start(part_hbm, part, sems.at[2]),
    ]
    unpack_into(packed, table)
    done = [start(table, table_hbm, sems.at[3])]
    finish(rest)
    for k, rows in enumerate(chunks(size)):
        sums = part[rows, :] + dot(adj[rows, :], table[...])
        pair = rows.start // 8
        pack(lane_tiles(sums), out, pair)
        here = pl.ds(pair, STEP // 8)
        done.append(start(out.at[here], out_hbm.at[here], sems.at[4 + k]))
    finish(done)


def own_first(
    rows_hbm, count_hbm, adj_hbm, table_hbm, live_hbm, x_hbm, w_hbm, v_hbm, b_hbm,
    rounded_hbm, degree_hbm, place_hbm, near_hbm, near_sums_hbm, near_degree_hbm, near_self_hbm,
    rows_v, count_v, adj, table, live, x, w, v, b, degree, place, near, near_sums, near_degree,
    near_self, pick, rounded, sems,
):
    nodes = x.shape[0]
    small = [start(rows_hbm, rows_v, sems.at[0]), start(count_hbm, count_v, sems.at[1])]
    loads = [
        start(adj_hbm.at[pl.ds(0, nodes)], adj, sems.at[2]),
        start(table_hbm, table, sems.at[3]),
        start(live_hbm, live, sems.at[4]),
        start(x_hbm, x, sems.at[5]),
        start(w_hbm, w, sems.at[6]),
        start(b_hbm, b, sems.at[7]),
        start(v_hbm, v, sems.at[13]),
    ]
    finish(small)
    slot = slot_rows(rows_v, count_v, 2 * nodes)
    fill_pick(slot, pick)
    done = []
    same = iota((128, 128), 0) == iota((128, 128), 1)
    for j in range(place.shape[1] // 128):
        lanes = slice(j * 128, (j + 1) * 128)
        wanted = jnp.sum(jnp.where(same, slot[lanes], 0.0), axis=0, keepdims=True)
        alike = jnp.logical_and(slot == wanted, slot < nodes)
        near[:, lanes] = jnp.where(alike, 1.0, 0.0).astype(BF)
        node = iota((nodes, 128), 0).astype(F32)
        place[:, lanes] = jnp.where(node == wanted, 1.0, 0.0).astype(BF)
    done.append(start(place, place_hbm, sems.at[9]))
    finish(loads)
    size = near.shape[0]
    done.append(start(v, near_hbm.at[:, pl.ds(size, v.shape[1])], sems.at[14]))
    ones = jnp.ones((nodes, 128), BF)
    for k, rows in enumerate(chunks(nodes)):
        total = (
            dot(adj[rows, :nodes], x[...]) + dot(adj[rows, nodes:], table[...]) + x[rows, :].astype(F32)
        )
        rounded[rows, :] = total.astype(BF)
        degree[rows, :] = dot(adj[rows, :nodes], ones) + dot(adj[rows, nodes:], live[...]) + 1.0
    done += [
        start(rounded, rounded_hbm, sems.at[10]),
        start(degree, degree_hbm, sems.at[11]),
    ]
    high = jnp.floor(degree[...] * (1.0 / 128.0))
    low = (degree[...] - 128.0 * high).astype(BF)
    high = high.astype(BF)
    for k, rows in enumerate(chunks(size)):
        dead = slot[rows] >= nodes
        mine = pick[rows, :]
        own_rows = dot(mine, x[...]).astype(BF)
        near_self[rows, :] = jnp.where(dead, -1e30, dot(own_rows, w[...]) + b[...])
        near_sums[rows, :] = dot(dot(mine, rounded[...]).astype(BF), v[...])
        near_degree[rows, :] = jnp.where(dead, 1.0, 128.0 * dot(mine, high) + dot(mine, low))
    done += [
        start(near, near_hbm.at[:, pl.ds(0, size)], sems.at[8]),
        start(near_sums, near_sums_hbm, sems.at[15]),
        start(near_degree, near_degree_hbm, sems.at[16]),
        start(near_self, near_self_hbm, sems.at[17]),
    ]
    finish(done)


def own_second(
    adj_hbm, table_hbm, x_hbm, inverse_hbm, w_hbm, v_hbm, b_hbm, self_hbm,
    adj, table, x, inverse, w, v, b, own_term, sems,
):
    nodes = x.shape[0]
    pairs = zip(
        (adj_hbm.at[pl.ds(0, nodes)], table_hbm, x_hbm, inverse_hbm, w_hbm, v_hbm, b_hbm),
        (adj, table, x, inverse, w, v, b),
    )
    finish([start(src, dst, sems.at[k]) for k, (src, dst) in enumerate(pairs)])
    done = []
    for k, rows in enumerate(chunks(nodes)):
        total = (
            dot(adj[rows, :nodes], x[...]) + dot(adj[rows, nodes:], table[...]) + x[rows, :].astype(F32)
        )
        mean = scaled(total, inverse[rows, :]).astype(BF)
        own_term[rows, :] = dot(x[rows, :], w[...]) + dot(mean, v[...]) + b[...]
        done.append(start(own_term.at[rows], self_hbm.at[rows], sems.at[7 + k]))
    finish(done)


def scaled(sums, inverse):
    return jnp.concatenate([tile * inverse for tile in lane_tiles(sums)], axis=1)


def layer_rows(select, mixed, degree, sums, own_term):
    width = own_term.shape[1]
    returned = dot(select, mixed)
    edges = returned[:, width:]
    other = pltpu.roll(edges, 64, 1)
    low = iota(edges.shape, 1) < 64
    scale = 1.0 / (degree + jnp.where(low, 128.0 * edges + other, edges + 128.0 * other))
    return jnp.maximum(own_term + scaled(sums + returned[:, :width], scale), 0.0), scale


def first_end(
    packed, degree_hbm, sums_hbm, self_hbm, near_hbm, mixed_hbm, out_hbm,
    degree, sums, w, own_term, near, back, mixed, out, sems,
):
    size, width = own_term.shape
    weights = start(near_hbm.at[:, pl.ds(size, width)], w, sems.at[0])
    need = [
        start(near_hbm.at[:, pl.ds(0, size)], near, sems.at[1]),
        start(degree_hbm, degree, sems.at[2]),
        start(sums_hbm, sums, sems.at[3]),
        start(self_hbm, own_term, sems.at[4]),
    ]
    for c in range(width // 128):
        back[:, c * 128 : (c + 1) * 128] = unpack_fours(packed, c).astype(BF)
    mixed[:, width:] = unpack_fours(packed, width // 128).astype(BF)
    weights.wait()
    mixed[:, :width] = dot(back[...], w[...]).astype(BF)
    done = [start(mixed, mixed_hbm.at[:, pl.ds(0, mixed.shape[1])], sems.at[5])]
    finish(need)
    for k, rows in enumerate(chunks(size)):
        hidden, _ = layer_rows(near[rows, :], mixed[...], degree[rows, :], sums[rows, :], own_term[rows, :])
        pair = rows.start // 8
        pack(lane_tiles(hidden), out, pair)
        here = pl.ds(pair, STEP // 8)
        done.append(start(out.at[here], out_hbm.at[here], sems.at[6 + k]))
    finish(done)


def hidden_rows(
    place_hbm, mixed_hbm, degree_hbm, rounded_hbm, x_hbm, w_hbm, v_hbm, b_hbm, adj_hbm,
    hidden_hbm, inverse_hbm, part_hbm,
    place, mixed, degree, rounded, x, w, v, b, adj, hidden, inverse, part, sems,
):
    size, own = adj.shape
    pairs = zip(
        (
            place_hbm, mixed_hbm.at[:, pl.ds(0, mixed.shape[1])], degree_hbm, rounded_hbm,
            x_hbm, w_hbm, v_hbm, b_hbm, adj_hbm.at[pl.ds(own, size), pl.ds(0, own)],
        ),
        (place, mixed, degree, rounded, x, w, v, b, adj),
    )
    finish([start(src, dst, sems.at[k]) for k, (src, dst) in enumerate(pairs)])
    for k, rows in enumerate(chunks(own)):
        value, inverse[rows, :] = layer_rows(
            place[rows, :], mixed[...], degree[rows, :],
            dot(rounded[rows, :], v[...]), dot(x[rows, :], w[...]) + b[...],
        )
        hidden[rows, :] = value.astype(BF)
    done = [start(hidden, hidden_hbm, sems.at[9]), start(inverse, inverse_hbm, sems.at[10])]
    for k, rows in enumerate(chunks(size)):
        part[rows, :] = dot(adj[rows, :], hidden[...])
    done.append(start(part, part_hbm, sems.at[11]))
    finish(done)


def second_end(
    packed, place_hbm, inverse_hbm, w_hbm, self_hbm, out_hbm,
    place, inverse, w, own_term, back, mixed, out, sems, self_sems,
):
    weights = start(w_hbm, w, sems.at[0])
    need = [start(place_hbm, place, sems.at[1]), start(inverse_hbm, inverse, sems.at[2])]
    steps = chunks(out.shape[0])
    own = [start(self_hbm.at[rows], own_term.at[rows], self_sems.at[k]) for k, rows in enumerate(steps)]
    unpack_into(packed, back)
    weights.wait()
    mixed[...] = dot(back[...], w[...]).astype(BF)
    finish(need)
    done = []
    for k, rows in enumerate(steps):
        returned = scaled(dot(place[rows, :], mixed[...]), inverse[rows, :])
        own[k].wait()
        out[rows, :] = (own_term[rows, :] + returned).astype(BF)
        done.append(start(out.at[rows], out_hbm.at[rows], sems.at[3 + k]))
    finish(done)


def array(*shape, dtype=F32):
    return jax.ShapeDtypeStruct(shape, dtype)


def call(kernel, outs, buffers, sems, flops, *in_specs):
    def run(*operands):
        held = [x for x, spec in zip(operands, in_specs) if spec is VMEM]
        room = sum(x.size * x.dtype.itemsize for x in held)
        spare = 200_000 if kernel is first_end else 0
        limit = ALL if kernel is first_gather else LIMIT - room - spare
        return pl.pallas_call(
            kernel,
            name=kernel.__name__,
            in_specs=list(in_specs) + [HBM] * (len(operands) - len(in_specs)),
            out_specs=[HBM] * len(outs),
            out_shape=list(outs),
            scratch_shapes=[pltpu.VMEM(b.shape, b.dtype) for b in buffers]
            + [pltpu.SemaphoreType.DMA((n,)) for n in sems],
            cost_estimate=pl.CostEstimate(flops=flops, bytes_accessed=4 << 20, transcendentals=0),
            compiler_params=pltpu.CompilerParams(vmem_limit_bytes=limit),
        )(*operands)

    return run


def exchange(packed):
    sent = packed.reshape((-1,) + packed.shape[2:])
    if packed.shape[3] == 8:
        sent = packed.reshape(sent.shape[0], -1, 128)
    arrived = lax.all_to_all(sent, "vert", split_axis=0, concat_axis=0, tiled=True)
    return arrived.reshape(packed.shape)


def body(
    features, send_rows, mirror_count, tile_coord, tile_mask, tile_count,
    w_self1, w_neigh1, bias1, w_self2, w_neigh2, bias2,
):
    own, width = features.shape
    _, peers, slots = send_rows.shape
    block = tile_mask.shape[2]
    tiles = tile_mask.shape[1]
    mirrors = peers * slots
    rows = own + mirrors
    pairs = peers // 2
    message = array(pairs, 2, 2, 8, 128, dtype=BF)
    longer = array(pairs, 2, 5, 4, 128, dtype=BF)
    nodes = array(own, width, dtype=BF)
    wide = array(own, width)
    narrow = array(own, 128)
    weight = array(width, width, dtype=BF)
    bias = array(1, width)
    table_a = array(mirrors, width, dtype=BF)
    live_a = array(mirrors, 128, dtype=BF)
    part_a = array(mirrors, width)
    edges_a = array(mirrors, 128)
    adj_a = array(rows, rows, dtype=BF)
    adj_own = array(own, rows, dtype=BF)
    adj_mirror = array(mirrors, mirrors, dtype=BF)
    adj_to_mirror = array(mirrors, own, dtype=BF)
    pick_a = array(mirrors, own, dtype=BF)
    place_a = array(own, mirrors, dtype=BF)
    slot_a = array(slots, peers, dtype=jnp.int32)
    count_a = array(1, peers, dtype=jnp.int32)

    slot_table = send_rows[0].T
    bias1 = bias1.astype(F32).reshape(1, width)
    bias2 = bias2.astype(F32).reshape(1, width)

    (sent,) = call(
        first_gather, [message], [slot_a, count_a, nodes, pick_a, message], [5],
        2 * mirrors * own * width,
    )(slot_table, mirror_count, features)
    arrived = exchange(sent)

    adj, part, edges = call(
        build_adjacency, [adj_a, part_a, edges_a],
        [array(tiles, block, block, dtype=jnp.int32), nodes, adj_a, part_a, edges_a],
        [tiles // GROUP, 4], 4 * rows * own * width, SMEM, SMEM,
    )(tile_coord[0], tile_count, tile_mask[0], features)

    table, live, sent = call(
        mirror_first, [table_a, live_a, longer],
        [adj_mirror, part_a, edges_a, table_a, live_a, longer], [8],
        2 * mirrors * mirrors * width, VMEM,
    )(arrived, adj, part, edges)
    arrived = exchange(sent)

    near_w = array(mirrors, mirrors + width, dtype=BF)
    rounded, degree, place, near, near_sums, near_degree, near_self = call(
        own_first, [nodes, narrow, place_a, near_w, part_a, edges_a, part_a],
        [
            slot_a, count_a, adj_own, table_a, live_a, nodes, weight, weight, bias,
            narrow, place_a, adj_mirror, part_a, edges_a, part_a, pick_a, nodes,
        ],
        [18], 6 * own * rows * width,
    )(slot_table, mirror_count, adj, table, live, features, w_self1, w_neigh1, bias1)

    mixed_a = array(mirrors, width + 128, dtype=BF)
    mixed, sent = call(
        first_end, [array(mirrors, 2 * width, dtype=BF), message],
        [edges_a, part_a, weight, part_a, adj_mirror, table_a, mixed_a, message], [8],
        4 * mirrors * mirrors * width, VMEM,
    )(arrived, near_degree, near_sums, near_self, near)
    arrived = exchange(sent)

    hidden, inverse, part = call(
        hidden_rows, [nodes, narrow, part_a],
        [
            place_a, mixed_a, narrow, nodes, nodes, weight, weight, bias, adj_to_mirror,
            nodes, narrow, part_a,
        ],
        [12], 4 * own * mirrors * width,
    )(place, mixed, degree, rounded, features, w_self1, w_neigh1, bias1, adj)

    table, sent = call(
        mirror_second, [table_a, message], [adj_mirror, part_a, table_a, message], [6],
        2 * mirrors * mirrors * width, VMEM,
    )(arrived, adj, part)
    arrived = exchange(sent)

    (own_term,) = call(
        own_second, [wide],
        [adj_own, table_a, nodes, narrow, weight, weight, bias, wide], [7 + own // STEP],
        4 * own * rows * width,
    )(adj, table, hidden, inverse, w_self2, w_neigh2, bias2)

    (embedding,) = call(
        second_end, [nodes],
        [place_a, narrow, weight, wide, table_a, table_a, nodes], [3 + own // STEP, own // STEP],
        4 * own * mirrors * width, VMEM,
    )(arrived, place, inverse, w_neigh2, own_term)
    return embedding


def solution(mesh):
    in_specs = (
        P("vert", None),
        P("vert", None, None),
        P("vert", None),
        P("vert", None, None),
        P("vert", None, None, None),
        P("vert"),
        P(),
        P(),
        P(),
        P(),
        P(),
        P(),
    )
    out_specs = P("vert", None)
    return jax.shard_map(body, mesh=mesh, in_specs=in_specs, out_specs=out_specs, check_vma=False)
```
